32 devices in a mesh: gx: 2 (over y), gy: 4 (over x, core), gz: 4 (over z).
Axes of the slice: x: 2, y: 2, z: 4, core: 2. Of those that a mesh axis runs over, the one named last changes fastest.
Arguments:
- tensor_blocks: bfloat16 [2, 4, 4, 3, 128, 128, 128], P('gx', 'gy', 'gz'), may hold values from 0 to 3
- fiber_mask: int32 [2, 4, 4, 3, 128, 128], P('gx', 'gy', 'gz'), may hold values 0 or 1
- block_coords: int32 [2, 4, 4, 3, 3], P('gx', 'gy', 'gz'), may hold values from 0 to 7, as said below
- block_counts: int32 [2, 4, 4], P('gx', 'gy', 'gz'), may hold values from 0 to 3, as said below
- factor_a: bfloat16 [2, 512, 256], P('gx', ('gy', 'gz')), may hold values from -0.59765625 to 0.59765625
- factor_b: bfloat16 [4, 1024, 256], P('gy', ('gx', 'gz')), may hold values from -0.59765625 to 0.59765625
- factor_c: bfloat16 [4, 512, 256], P('gz', ('gx', 'gy')), may hold values from -0.59765625 to 0.59765625
Outputs:
- grad_a: float32 [2, 512, 256], P('gx', ('gy', 'gz'))
- grad_b: float32 [4, 1024, 256], P('gy', ('gx', 'gz'))
- grad_c: float32 [4, 512, 256], P('gz', ('gx', 'gy'))
The draws below stay inside these ranges and needn't reach their ends.
Inputs may be any that keep to these rules, and one draw needn't show every extreme that they name: `block_counts`: some sub-box holds exactly 3 blocks and some holds none, in every draw; slots at and past a sub-box's count hold no block. `block_coords`: the 3 columns of one sub-box name distinct blocks; row 0 is below 4, row 1 below 8, row 2 below 4.
All inputs are finite; a program needn't handle non-finite values. No bound on the sum of `fiber_mask` on one device may be relied on, other than what follows from the above.
Results may differ from the reference program's by a relative error of at most 0.0014.
Values may be sent and summed in bfloat16 or wider, within the bound.
No kernel may reach another device: no remote copies, remote signals or barrier semaphores. Data moves between devices by JAX's collectives and lax.ppermute only.
A program may use at most 128 MiB of HBM per device.

```python
import jax
import jax.numpy as jnp
from jax import lax

R = 256
BLK = 128
SLOTS = 3
BX = 4
BY = 8
BZ = 4
SA = 512
SB = 1024
SC = 512
N_GX = 2
N_GY = 4
N_GZ = 4


def draw_block_counts(key, part):
    total = N_GX * N_GY * N_GZ
    first, second, third = jax.random.split(jax.random.fold_in(key, 11), 3)
    raw = jax.random.randint(first, (total,), 0, 5)
    table = jnp.array([0, 1, 1, 2, 3], jnp.int32)
    counts = jnp.minimum(table[raw], SLOTS)
    busiest = jax.random.randint(second, (), 0, total)
    emptiest = (busiest + 1 + jax.random.randint(third, (), 0, total - 1)) % total
    counts = counts.at[busiest].set(SLOTS).at[emptiest].set(0)
    return counts.reshape(N_GX, N_GY, N_GZ).astype(jnp.int32)


def draw_block_coords(key, part):
    total = N_GX * N_GY * N_GZ
    cells = BX * BY * BZ
    scores = jax.random.randint(jax.random.fold_in(key, 23), (total, cells), 0, 2 ** 30 // cells)
    scores = scores * cells + jnp.arange(cells, dtype=jnp.int32)[None, :]
    picks = jnp.argsort(-scores, axis=1)[:, :SLOTS].astype(jnp.int32)
    first = picks // (BY * BZ)
    second = picks // BZ % BY
    third = picks % BZ
    coords = jnp.stack([first, second, third], axis=1)
    return coords.reshape(N_GX, N_GY, N_GZ, 3, SLOTS).astype(jnp.int32)


def plant(values, rng, smallest, high):
    longest = values.shape.index(max(values.shape))
    spots = []
    for shift in (0, 1):
        where = [jax.random.randint(jax.random.fold_in(rng, axis), (), 0, length) for axis, length in enumerate(values.shape)]
        where[longest] = (where[longest] + shift) % values.shape[longest]
        spots.append(tuple(where))
    return values.at[spots[0]].set(smallest).at[spots[1]].set(high)


def levels(stream_key, dims, cuts, smallest, top_value):
    def one(position, shards_of):
        draws = jax.random.uniform(jax.random.fold_in(jax.random.fold_in(stream_key, 6), position), (shards_of,), jnp.float32, smallest / len(cuts), top_value / len(cuts))
        return jnp.repeat(jnp.exp(draws), dims[position] // shards_of).reshape((-1,) + (1,) * (len(dims) - position - 1))

    loudness = one(*cuts[0])
    for cut in cuts[1:]:
        loudness = loudness * one(*cut)
    return loudness


def setup_inputs(seed: int = 0) -> dict:
    streams_of = jax.random.split(jax.random.key(seed), 8)
    return {
        "tensor_blocks": jnp.clip(3.0 * jax.random.uniform(streams_of[0], (N_GX, N_GY, N_GZ, SLOTS, BLK, BLK, BLK), jnp.float32) ** levels(streams_of[0], (N_GX, N_GY, N_GZ, SLOTS, BLK, BLK, BLK), ((0, 2), (1, 4), (2, 4)), -0.2, 0.2), 0.0, 3.0).astype(jnp.bfloat16),
        "fiber_mask": plant((jax.random.randint(streams_of[1], (N_GX, N_GY, N_GZ, SLOTS, BLK, BLK), 0, 4) < 3).astype(jnp.int32), jax.random.fold_in(streams_of[1], 1), 0, 1),
        "block_coords": draw_block_coords(jax.random.fold_in(streams_of[7], 71), 0),
        "block_counts": draw_block_counts(jax.random.fold_in(streams_of[7], 71), 0),
        "factor_a": jnp.clip(jax.random.uniform(streams_of[4], (N_GX, SA, R), jnp.float32, -0.59765625, 0.59765625) * levels(streams_of[4], (N_GX, SA, R), ((0, 2), (1, 16)), -0.4, 0.0), -0.59765625, 0.59765625).astype(jnp.bfloat16),
        "factor_b": jnp.clip(jax.random.uniform(streams_of[5], (N_GY, SB, R), jnp.float32, -0.59765625, 0.59765625) * levels(streams_of[5], (N_GY, SB, R), ((0, 4), (1, 8)), -0.4, 0.0), -0.59765625, 0.59765625).astype(jnp.bfloat16),
        "factor_c": jnp.clip(jax.random.uniform(streams_of[6], (N_GZ, SC, R), jnp.float32, -0.59765625, 0.59765625) * levels(streams_of[6], (N_GZ, SC, R), ((0, 4), (1, 8)), -0.4, 0.0), -0.59765625, 0.59765625).astype(jnp.bfloat16),
    }


def block_terms(rows_a, rows_b, rows_c, entries, fibers):
    khatri = (rows_b[:, None, :].astype(jnp.float32) * rows_c[None, :, :].astype(jnp.float32)).astype(jnp.bfloat16)
    khatri = khatri.reshape(BLK * BLK, R)
    log_rate = jnp.dot(rows_a, khatri.T, preferred_element_type=jnp.float32)
    weight = fibers.astype(jnp.float32).reshape(BLK, BLK, 1)
    misfit = weight * (jnp.exp(log_rate.reshape(BLK, BLK, BLK)) - entries.astype(jnp.float32)) / BLK
    misfit = misfit.astype(jnp.bfloat16).reshape(BLK, BLK * BLK)
    part_a = jnp.dot(misfit, khatri, preferred_element_type=jnp.float32)
    folded = jnp.einsum("uk,ur->kr", misfit.astype(jnp.float32), rows_a.astype(jnp.float32))
    folded = folded.astype(jnp.bfloat16).reshape(BLK, BLK, R)
    part_b = jnp.einsum("vwr,wr->vr", folded.astype(jnp.float32), rows_c.astype(jnp.float32))
    part_c = jnp.einsum("vwr,vr->wr", folded.astype(jnp.float32), rows_b.astype(jnp.float32))
    return part_a, part_b, part_c


def add_rows(total, slab, start, part):
    anchor = jnp.zeros((), jnp.int32)
    current = lax.dynamic_slice(total, (slab.astype(jnp.int32), start.astype(jnp.int32), anchor), (1, BLK, R))
    return lax.dynamic_update_slice(total, current + part[None].astype(total.dtype),
                                    (slab.astype(jnp.int32), start.astype(jnp.int32), anchor))


def reference(tensor_blocks, fiber_mask, block_coords, block_counts, factor_a, factor_b, factor_c):
    def advance(totals, flat_index):
        flat_index = flat_index.astype(jnp.int32)
        device = (flat_index // SLOTS).astype(jnp.int32)
        slot_index = (flat_index % SLOTS).astype(jnp.int32)
        mode_one = (device // (N_GY * N_GZ)).astype(jnp.int32)
        mode_two = ((device // N_GZ) % N_GY).astype(jnp.int32)
        mode_three = (device % N_GZ).astype(jnp.int32)
        filled = block_counts[mode_one, mode_two, mode_three]

        def accumulate(totals):
            grad_a, grad_b, grad_c = totals
            anchor = jnp.zeros((), jnp.int32)
            coords = block_coords[mode_one, mode_two, mode_three]
            start_a = (coords[0, slot_index] * BLK).astype(jnp.int32)
            start_b = (coords[1, slot_index] * BLK).astype(jnp.int32)
            start_c = (coords[2, slot_index] * BLK).astype(jnp.int32)
            rows_a = lax.dynamic_slice(factor_a, (mode_one, start_a, anchor), (1, BLK, R))[0]
            rows_b = lax.dynamic_slice(factor_b, (mode_two, start_b, anchor), (1, BLK, R))[0]
            rows_c = lax.dynamic_slice(factor_c, (mode_three, start_c, anchor), (1, BLK, R))[0]
            entries = tensor_blocks[mode_one, mode_two, mode_three, slot_index]
            fibers = fiber_mask[mode_one, mode_two, mode_three, slot_index]
            part_a, part_b, part_c = block_terms(rows_a, rows_b, rows_c, entries, fibers)
            return (add_rows(grad_a, mode_one, start_a, part_a),
                    add_rows(grad_b, mode_two, start_b, part_b),
                    add_rows(grad_c, mode_three, start_c, part_c))

        return lax.cond(slot_index < filled, accumulate, lambda kept: kept, totals), None

    start = (jnp.zeros(factor_a.shape, jnp.float32), jnp.zeros(factor_b.shape, jnp.float32),
             jnp.zeros(factor_c.shape, jnp.float32))
    totals, _ = lax.scan(advance, start, jnp.arange(N_GX * N_GY * N_GZ * SLOTS, dtype=jnp.int32))
    return totals[0], totals[1], totals[2]
```

```python
import functools

import jax
import jax.numpy as jnp
from jax import lax
from jax.experimental import pallas as pl
from jax.experimental.pallas import tpu as pltpu
from jax.sharding import PartitionSpec as P

BLK = 128
STEP = 64
GROUP = 8
PAD = 16
TOP = 32000.0


def pack(parts, target):
    at, powers = 0, []
    for part in parts:
        largest = jnp.maximum(jnp.max(jnp.abs(part), 0, keepdims=True), 1e-33)
        power = jnp.clip(jnp.ceil(jnp.log2(largest * (1.0 / TOP))), -120.0, 120.0)
        values = jnp.round(part * jnp.exp2(-power)).astype(jnp.int32)
        target[at : at + part.shape[0], :] = values.astype(jnp.int16)
        powers.append(power.astype(jnp.int32))
        at += part.shape[0]
    fill = jnp.zeros((PAD - len(powers), powers[0].shape[1]), jnp.int32)
    target[at : at + PAD, :] = jnp.concatenate([*powers, fill], 0).astype(jnp.int16)


def unpack(source, sizes):
    at, parts = 0, []
    powers = source[sum(sizes) : sum(sizes) + PAD, :].astype(jnp.int32).astype(jnp.float32)
    for i, size in enumerate(sizes):
        values = source[at : at + size, :].astype(jnp.int32).astype(jnp.float32)
        parts.append(values * jnp.exp2(powers[i : i + 1, :]))
        at += size
    return parts


def block_kernel(nx, ny, nz, filled, coords, entries, *refs):
    n_bc, n_a = nx, ny
    got_bc, got_a = refs[:n_bc], refs[n_bc : n_bc + n_a]
    refs = refs[n_bc + n_a :]
    own_bc, own_a = refs[:2]
    send_bc, send_a = refs[2 : 2 + nx - 1], refs[1 + nx : nx + ny]
    slab_a, slab_b, slab_c, grad_a, grad_b, grad_c = refs[nx + ny :]
    x, y, z = (lax.axis_index(name) for name in ("gx", "gy", "gz"))
    rank = slab_a.shape[1]
    all_a, all_b, all_c = (s.shape[0] for s in (slab_a, slab_b, slab_c))
    per_a, per_b, per_c = all_a // (ny * nz), all_b // (nx * nz), all_c // (nx * ny)
    slot, step = pl.program_id(0), pl.program_id(1)

    @pl.when((slot == 0) & (step == 0))
    def _():
        grad_a[...] = jnp.zeros_like(grad_a)
        grad_b[...] = jnp.zeros_like(grad_b)
        grad_c[...] = jnp.zeros_like(grad_c)
        for i in range(nx):
            of_x = lax.rem(x + nx - i, nx)
            for j in range(nz):
                at = (of_x * nz + lax.rem(z + nz - j, nz)) * per_b
                slab_b[pl.ds(pl.multiple_of(at, per_b), per_b), :] = got_bc[i][j * per_b : (j + 1) * per_b, :]
            for j in range(ny):
                at = (of_x * ny + lax.rem(y + ny - j, ny)) * per_c
                first = nz * per_b + j * per_c
                slab_c[pl.ds(pl.multiple_of(at, per_c), per_c), :] = got_bc[i][first : first + per_c, :]
        for i in range(ny):
            of_y = lax.rem(y + ny - i, ny)
            for j in range(nz):
                at = (of_y * nz + lax.rem(z + nz - j, nz)) * per_a
                slab_a[pl.ds(pl.multiple_of(at, per_a), per_a), :] = got_a[i][j * per_a : (j + 1) * per_a, :]

    @pl.when(slot < filled[0, 0, 0])
    def _():
        at_a = pl.multiple_of(coords[0, 0, 0, 0, slot] * BLK + step * STEP, STEP)
        at_b = pl.multiple_of(coords[0, 0, 0, 1, slot] * BLK, BLK)
        at_c = pl.multiple_of(coords[0, 0, 0, 2, slot] * BLK, BLK)
        rows_a = slab_a[pl.ds(at_a, STEP), :].astype(jnp.float32)
        rows_b = slab_b[pl.ds(at_b, BLK), :]
        rows_c = slab_c[pl.ds(at_c, BLK), :]
        wide_b = rows_b.astype(jnp.float32)
        sum_b = jnp.zeros((BLK, rank), jnp.float32)
        sum_c = jnp.zeros((BLK, rank), jnp.float32)
        parts = []
        for first in range(0, STEP, GROUP):
            mixed = []
            for u in range(first, first + GROUP):
                row = jnp.broadcast_to(rows_a[u : u + 1, :], (16, rank)).astype(jnp.bfloat16)
                mixed.append((rows_b.reshape(BLK // 16, 16, rank) * row[None]).reshape(BLK, rank))
            mixed = jnp.concatenate(mixed, 0)
            rate = lax.dot_general(mixed, rows_c, (((1,), (1,)), ((), ())), preferred_element_type=jnp.float32)
            seen = entries[0, first : first + GROUP].reshape(GROUP * BLK, BLK).astype(jnp.float32)
            error = jnp.where(seen < 0, 0.0, jnp.exp(rate) - seen).astype(jnp.bfloat16)
            spread = jnp.dot(error, rows_c, preferred_element_type=jnp.float32)
            for i in range(GROUP):
                mine = spread[i * BLK : (i + 1) * BLK]
                sum_b = sum_b + mine * rows_a[first + i : first + i + 1, :]
                parts.append(jnp.sum(mine * wide_b, 0, keepdims=True))
            sum_c = sum_c + lax.dot_general(
                error, mixed, (((0,), (0,)), ((), ())), preferred_element_type=jnp.float32
            )
        grad_a[pl.ds(at_a, STEP), :] += jnp.concatenate(parts, 0)
        grad_b[pl.ds(at_b, BLK), :] += sum_b
        grad_c[pl.ds(at_c, BLK), :] += sum_c

    @pl.when((slot == pl.num_programs(0) - 1) & (step == pl.num_programs(1) - 1))
    def _():
        some_b, some_c, some_a = all_b // nx, all_c // nx, all_a // ny
        for i in range(nx):
            to_x = lax.rem(x + i, nx)
            part_b = grad_b[pl.ds(pl.multiple_of(to_x * some_b, some_b), some_b), :]
            part_c = grad_c[pl.ds(pl.multiple_of(to_x * some_c, some_c), some_c), :]
            if i == 0:
                own_bc[:some_b, :] = part_b
                own_bc[some_b:, :] = part_c
            else:
                pack((part_b, part_c), send_bc[i - 1])
        for i in range(ny):
            to_y = lax.rem(y + i, ny)
            part_a = grad_a[pl.ds(pl.multiple_of(to_y * some_a, some_a), some_a), :]
            if i == 0:
                own_a[...] = part_a
            else:
                pack((part_a,), send_a[i - 1])


def whole(array):
    zeros = (0,) * len(array.shape)
    return pl.BlockSpec(array.shape, lambda *_: zeros)


def middle_kernel(nx, ny, nz, sizes, *refs):
    some_b, some_c, some_a = sizes
    own_bc, own_a = refs[:2]
    got_bc, got_a = refs[2 : 1 + nx], refs[1 + nx : nx + ny]
    own_ba, own_c = refs[nx + ny : nx + ny + 2]
    send_ba = refs[nx + ny + 2 : nx + ny + 1 + nz]
    send_c = refs[nx + ny + 1 + nz : nx + 2 * ny + nz]
    sum_b, sum_c, sum_a = refs[nx + 2 * ny + nz :]
    y, z = lax.axis_index("gy"), lax.axis_index("gz")
    total_b, total_c, total_a = own_bc[:some_b, :], own_bc[some_b:, :], own_a[...]
    for ref in got_bc:
        part_b, part_c = unpack(ref, (some_b, some_c))
        total_b, total_c = total_b + part_b, total_c + part_c
    for ref in got_a:
        total_a = total_a + unpack(ref, (some_a,))[0]
    sum_b[...], sum_c[...], sum_a[...] = total_b, total_c, total_a
    per_b, per_c, per_a = some_b // nz, some_c // ny, some_a // nz
    for i in range(nz):
        to_z = lax.rem(z + i, nz)
        part_b = sum_b[pl.ds(pl.multiple_of(to_z * per_b, per_b), per_b), :]
        part_a = sum_a[pl.ds(pl.multiple_of(to_z * per_a, per_a), per_a), :]
        if i == 0:
            own_ba[:per_b, :] = part_b
            own_ba[per_b:, :] = part_a
        else:
            pack((part_b, part_a), send_ba[i - 1])
    for i in range(ny):
        to_y = lax.rem(y + i, ny)
        part_c = sum_c[pl.ds(pl.multiple_of(to_y * per_c, per_c), per_c), :]
        if i == 0:
            own_c[...] = part_c
        else:
            pack((part_c,), send_c[i - 1])


def last_kernel(ny, nz, sizes, *refs):
    per_b, per_c, per_a = sizes
    own_ba, own_c = refs[:2]
    got_ba, got_c = refs[2 : 1 + nz], refs[1 + nz : nz + ny]
    grad_a, grad_b, grad_c = refs[nz + ny :]
    total_b, total_a, total_c = own_ba[:per_b, :], own_ba[per_b:, :], own_c[...]
    for ref in got_ba:
        part_b, part_a = unpack(ref, (per_b, per_a))
        total_b, total_a = total_b + part_b, total_a + part_a
    for ref in got_c:
        total_c = total_c + unpack(ref, (per_c,))[0]
    grad_a[0] = total_a * (1.0 / BLK)
    grad_b[0] = total_b * (1.0 / BLK)
    grad_c[0] = total_c * (1.0 / BLK)


def shift(array, axis, size, by):
    return lax.ppermute(array, axis, [(i, (i + by) % size) for i in range(size)])


def around(array, axis, size):
    return [array] + [shift(array, axis, size, by) for by in range(1, size)]


def per_device(nx, ny, nz, tensor_blocks, fiber_mask, block_coords, block_counts, factor_a, factor_b, factor_c):
    per_a, per_b, per_c = (f.shape[1] for f in (factor_a, factor_b, factor_c))
    rank = factor_a.shape[2]
    all_a, all_b, all_c = per_a * ny * nz, per_b * nx * nz, per_c * nx * ny
    some_a, some_b, some_c = per_a * nz, per_b * nz, per_c * ny
    slots = tensor_blocks.shape[3]

    entries = jnp.where(fiber_mask[0, 0, 0][..., None] != 0, tensor_blocks[0, 0, 0], -1)

    along_z = around(jnp.concatenate([factor_b[0], factor_a[0]], 0), "gz", nz)
    along_y = around(factor_c[0], "gy", ny)
    half_bc = jnp.concatenate([p[:per_b] for p in along_z] + along_y, 0)
    some_rows_a = jnp.concatenate([p[per_b:] for p in along_z], 0)
    got_bc = around(half_bc, "gx", nx)
    got_a = around(some_rows_a, "gy", ny)

    def where(slot, step, filled, coords):
        held = filled[0, 0, 0]
        last = jnp.maximum(held - 1, 0)
        return (jnp.minimum(slot, last), jnp.where(slot < held, step, BLK // STEP - 1), 0, 0)

    f32, i16 = jnp.float32, jnp.int16
    outs = [jax.ShapeDtypeStruct((some_b + some_c, rank), f32), jax.ShapeDtypeStruct((some_a, rank), f32)]
    outs += [jax.ShapeDtypeStruct((some_b + some_c + PAD, rank), i16)] * (nx - 1)
    outs += [jax.ShapeDtypeStruct((some_a + PAD, rank), i16)] * (ny - 1)
    results = pl.pallas_call(
        functools.partial(block_kernel, nx, ny, nz),
        grid_spec=pltpu.PrefetchScalarGridSpec(
            num_scalar_prefetch=2,
            grid=(slots, BLK // STEP),
            in_specs=[pl.BlockSpec((1, STEP, BLK, BLK), where), *map(whole, got_bc), *map(whole, got_a)],
            out_specs=[*map(whole, outs)],
            scratch_shapes=[pltpu.VMEM((n, rank), jnp.bfloat16) for n in (all_a, all_b, all_c)]
            + [pltpu.VMEM((n, rank), f32) for n in (all_a, all_b, all_c)],
        ),
        out_shape=outs,
        compiler_params=pltpu.CompilerParams(
            vmem_limit_bytes=40 * 2**20, dimension_semantics=("arbitrary", "arbitrary")
        ),
        name="blocks",
    )(block_counts, block_coords, entries, *got_bc, *got_a)

    own_bc, own_a = results[:2]
    got_bc = [shift(r, "gx", nx, i + 1) for i, r in enumerate(results[2 : 1 + nx])]
    got_a = [shift(r, "gy", ny, i + 1) for i, r in enumerate(results[1 + nx :])]
    outs = [jax.ShapeDtypeStruct((per_b + per_a, rank), f32), jax.ShapeDtypeStruct((per_c, rank), f32)]
    outs += [jax.ShapeDtypeStruct((per_b + per_a + PAD, rank), i16)] * (nz - 1)
    outs += [jax.ShapeDtypeStruct((per_c + PAD, rank), i16)] * (ny - 1)
    results = pl.pallas_call(
        functools.partial(middle_kernel, nx, ny, nz, (some_b, some_c, some_a)),
        out_shape=outs,
        scratch_shapes=[pltpu.VMEM((n, rank), f32) for n in (some_b, some_c, some_a)],
        compiler_params=pltpu.CompilerParams(vmem_limit_bytes=32 * 2**20),
        name="middle",
    )(own_bc, own_a, *got_bc, *got_a)

    own_ba, own_c = results[:2]
    got_ba = [shift(r, "gz", nz, i + 1) for i, r in enumerate(results[2 : 1 + nz])]
    got_c = [shift(r, "gy", ny, i + 1) for i, r in enumerate(results[1 + nz :])]
    return pl.pallas_call(
        functools.partial(last_kernel, ny, nz, (per_b, per_c, per_a)),
        out_shape=[jax.ShapeDtypeStruct((1, n, rank), f32) for n in (per_a, per_b, per_c)],
        compiler_params=pltpu.CompilerParams(vmem_limit_bytes=32 * 2**20),
        name="last",
    )(own_ba, own_c, *got_ba, *got_c)


def solution(mesh):
    nx, ny, nz = (mesh.shape[name] for name in ("gx", "gy", "gz"))
    placed = (
        P("gx", "gy", "gz", None, None, None, None),
        P("gx", "gy", "gz", None, None, None),
        P("gx", "gy", "gz", None, None),
        P("gx", "gy", "gz"),
        P("gx", ("gy", "gz"), None),
        P("gy", ("gx", "gz"), None),
        P("gz", ("gx", "gy"), None),
    )
    return jax.shard_map(
        functools.partial(per_device, nx, ny, nz),
        mesh=mesh,
        in_specs=placed,
        out_specs=(
            P("gx", ("gy", "gz"), None),
            P("gy", ("gx", "gz"), None),
            P("gz", ("gx", "gy"), None),
        ),
        check_vma=False,
    )
```

```python
import functools

import jax
import jax.numpy as jnp
from jax import lax
from jax.experimental import pallas as pl
from jax.experimental.pallas import tpu as pltpu
from jax.sharding import PartitionSpec as P

BLK = 128
STEP = 64
GROUP = 8
PAD = 16
TOP = 32000.0


def pack(parts, target):
    at, powers = 0, []
    for part in parts:
        largest = jnp.maximum(jnp.max(jnp.abs(part), 0, keepdims=True), 1e-33)
        power = jnp.clip(jnp.ceil(jnp.log2(largest * (1.0 / TOP))), -120.0, 120.0)
        values = jnp.round(part * jnp.exp2(-power)).astype(jnp.int32)
        target[at : at + part.shape[0], :] = values.astype(jnp.int16)
        powers.append(power.astype(jnp.int32))
        at += part.shape[0]
    fill = jnp.zeros((PAD - len(powers), powers[0].shape[1]), jnp.int32)
    target[at : at + PAD, :] = jnp.concatenate([*powers, fill], 0).astype(jnp.int16)


def unpack(source, sizes):
    at, parts = 0, []
    powers = source[sum(sizes) : sum(sizes) + PAD, :].astype(jnp.int32).astype(jnp.float32)
    for i, size in enumerate(sizes):
        values = source[at : at + size, :].astype(jnp.int32).astype(jnp.float32)
        parts.append(values * jnp.exp2(powers[i : i + 1, :]))
        at += size
    return parts


def block_kernel(nx, ny, nz, filled, coords, entries, fibers, *refs):
    got_b, got_ac = refs[:nx], refs[nx : nx + ny]
    refs = refs[nx + ny :]
    own_b, own_ac = refs[:2]
    send_b, send_ac = refs[2 : 1 + nx], refs[1 + nx : nx + ny]
    slab_a, slab_b, slab_c, grad_a, grad_b, grad_c = refs[nx + ny :]
    x, y, z = (lax.axis_index(name) for name in ("gx", "gy", "gz"))
    rank = slab_a.shape[1]
    all_a, all_b, all_c = (s.shape[0] for s in (slab_a, slab_b, slab_c))
    per_a, per_b, per_c = all_a // (ny * nz), all_b // (nx * nz), all_c // (nx * ny)
    slot, step = pl.program_id(0), pl.program_id(1)

    @pl.when((slot == 0) & (step == 0))
    def _():
        grad_a[...] = jnp.zeros_like(grad_a)
        grad_b[...] = jnp.zeros_like(grad_b)
        grad_c[...] = jnp.zeros_like(grad_c)
        for j in range(nz):
            of_z = lax.rem(z + nz - j, nz)
            for i in range(nx):
                at = (lax.rem(x + nx - i, nx) * nz + of_z) * per_b
                slab_b[pl.ds(pl.multiple_of(at, per_b), per_b), :] = got_b[i][j * per_b : (j + 1) * per_b, :]
            for i in range(ny):
                at = (lax.rem(y + ny - i, ny) * nz + of_z) * per_a
                slab_a[pl.ds(pl.multiple_of(at, per_a), per_a), :] = got_ac[i][j * per_a : (j + 1) * per_a, :]
        for j in range(nx):
            of_x = lax.rem(x + nx - j, nx)
            for i in range(ny):
                at = (of_x * ny + lax.rem(y + ny - i, ny)) * per_c
                first = nz * per_a + j * per_c
                slab_c[pl.ds(pl.multiple_of(at, per_c), per_c), :] = got_ac[i][first : first + per_c, :]

    @pl.when(slot < filled[0, 0, 0])
    def _():
        at_a = pl.multiple_of(coords[0, 0, 0, 0, slot] * BLK + step * STEP, STEP)
        at_b = pl.multiple_of(coords[0, 0, 0, 1, slot] * BLK, BLK)
        at_c = pl.multiple_of(coords[0, 0, 0, 2, slot] * BLK, BLK)
        rows_a = slab_a[pl.ds(at_a, STEP), :].astype(jnp.float32)
        rows_b = slab_b[pl.ds(at_b, BLK), :]
        rows_c = slab_c[pl.ds(at_c, BLK), :]
        wide_b = rows_b.astype(jnp.float32)
        sum_b = jnp.zeros((BLK, rank), jnp.float32)
        sum_c = jnp.zeros((BLK, rank), jnp.float32)
        parts = []
        weight = jnp.transpose(fibers[0, 0, 0, 0].astype(jnp.float32)).astype(jnp.bfloat16)
        for first in range(0, STEP, GROUP):
            mixed = []
            for u in range(first, first + GROUP):
                row = jnp.broadcast_to(rows_a[u : u + 1, :], (16, rank)).astype(jnp.bfloat16)
                mixed.append((rows_b.reshape(BLK // 16, 16, rank) * row[None]).reshape(BLK, rank))
            mixed = jnp.concatenate(mixed, 0)
            rate = lax.dot_general(mixed, rows_c, (((1,), (1,)), ((), ())), preferred_element_type=jnp.float32)
            seen = entries[0, 0, 0, 0, first : first + GROUP].reshape(GROUP * BLK, BLK).astype(jnp.float32)
            error = (jnp.exp(rate) - seen).astype(jnp.bfloat16)
            error = [
                error[i * BLK : (i + 1) * BLK] * weight[:, first + i : first + i + 1] for i in range(GROUP)
            ]
            error = jnp.concatenate(error, 0)
            spread = jnp.dot(error, rows_c, preferred_element_type=jnp.float32)
            for i in range(GROUP):
                mine = spread[i * BLK : (i + 1) * BLK]
                sum_b = sum_b + mine * rows_a[first + i : first + i + 1, :]
                parts.append(jnp.sum(mine * wide_b, 0, keepdims=True))
            sum_c = sum_c + lax.dot_general(
                error, mixed, (((0,), (0,)), ((), ())), preferred_element_type=jnp.float32
            )
        grad_a[pl.ds(at_a, STEP), :] += jnp.concatenate(parts, 0)
        grad_b[pl.ds(at_b, BLK), :] += sum_b
        grad_c[pl.ds(at_c, BLK), :] += sum_c

    @pl.when((slot == pl.num_programs(0) - 1) & (step == pl.num_programs(1) - 1))
    def _():
        some_b, some_a = all_b // nx, all_a // ny
        for i in range(nx):
            to_x = lax.rem(x + i, nx)
            part_b = grad_b[pl.ds(pl.multiple_of(to_x * some_b, some_b), some_b), :]
            if i == 0:
                own_b[...] = part_b
            else:
                pack((part_b,), send_b[i - 1])
        for i in range(ny):
            to_y = lax.rem(y + i, ny)
            part_a = grad_a[pl.ds(pl.multiple_of(to_y * some_a, some_a), some_a), :]
            part_c = jnp.concatenate(
                [grad_c[pl.ds(pl.multiple_of((j * ny + to_y) * per_c, per_c), per_c), :] for j in range(nx)], 0
            )
            if i == 0:
                own_ac[:some_a, :] = part_a
                own_ac[some_a:, :] = part_c
            else:
                pack((part_a, part_c), send_ac[i - 1])


def whole(array):
    zeros = (0,) * len(array.shape)
    return pl.BlockSpec(array.shape, lambda *_: zeros)


def middle_kernel(nx, ny, nz, sizes, *refs):
    some_b, some_c, some_a = sizes
    own_b, own_ac = refs[:2]
    got_b, got_ac = refs[2 : 1 + nx], refs[1 + nx : nx + ny]
    own_ba, own_c = refs[nx + ny : nx + ny + 2]
    send_ba = refs[nx + ny + 2 : nx + ny + 1 + nz]
    send_c = refs[nx + ny + 1 + nz : 2 * nx + ny + nz]
    sum_b, sum_c, sum_a = refs[2 * nx + ny + nz :]
    x, z = lax.axis_index("gx"), lax.axis_index("gz")
    total_b, total_a, total_c = own_b[...], own_ac[:some_a, :], own_ac[some_a:, :]
    for ref in got_b:
        total_b = total_b + unpack(ref, (some_b,))[0]
    for ref in got_ac:
        part_a, part_c = unpack(ref, (some_a, some_c))
        total_a, total_c = total_a + part_a, total_c + part_c
    sum_b[...], sum_c[...], sum_a[...] = total_b, total_c, total_a
    per_b, per_c, per_a = some_b // nz, some_c // nx, some_a // nz
    for i in range(nz):
        to_z = lax.rem(z + i, nz)
        part_b = sum_b[pl.ds(pl.multiple_of(to_z * per_b, per_b), per_b), :]
        part_a = sum_a[pl.ds(pl.multiple_of(to_z * per_a, per_a), per_a), :]
        if i == 0:
            own_ba[:per_b, :] = part_b
            own_ba[per_b:, :] = part_a
        else:
            pack((part_b, part_a), send_ba[i - 1])
    for i in range(nx):
        to_x = lax.rem(x + i, nx)
        part_c = sum_c[pl.ds(pl.multiple_of(to_x * per_c, per_c), per_c), :]
        if i == 0:
            own_c[...] = part_c
        else:
            pack((part_c,), send_c[i - 1])


def last_kernel(nx, nz, sizes, *refs):
    per_b, per_c, per_a = sizes
    own_ba, own_c = refs[:2]
    got_ba, got_c = refs[2 : 1 + nz], refs[1 + nz : nz + nx]
    grad_a, grad_b, grad_c = refs[nz + nx :]
    total_b, total_a, total_c = own_ba[:per_b, :], own_ba[per_b:, :], own_c[...]
    for ref in got_ba:
        part_b, part_a = unpack(ref, (per_b, per_a))
        total_b, total_a = total_b + part_b, total_a + part_a
    for ref in got_c:
        total_c = total_c + unpack(ref, (per_c,))[0]
    grad_a[0] = total_a * (1.0 / BLK)
    grad_b[0] = total_b * (1.0 / BLK)
    grad_c[0] = total_c * (1.0 / BLK)


def shift(array, axis, size, by):
    return lax.ppermute(array, axis, [(i, (i + by) % size) for i in range(size)])


def around(array, axis, size):
    return [array] + [shift(array, axis, size, by) for by in range(1, size)]


def per_device(nx, ny, nz, tensor_blocks, fiber_mask, block_coords, block_counts, factor_a, factor_b, factor_c):
    per_a, per_b, per_c = (f.shape[1] for f in (factor_a, factor_b, factor_c))
    rank = factor_a.shape[2]
    all_a, all_b, all_c = per_a * ny * nz, per_b * nx * nz, per_c * nx * ny
    some_a, some_b, some_c = per_a * nz, per_b * nz, per_c * nx
    slots = tensor_blocks.shape[3]

    along_z = around(jnp.concatenate([factor_b[0], factor_a[0]], 0), "gz", nz)
    along_x = around(factor_c[0], "gx", nx)
    got_b = around(jnp.concatenate([p[:per_b] for p in along_z], 0), "gx", nx)
    got_ac = around(jnp.concatenate([p[per_b:] for p in along_z] + along_x, 0), "gy", ny)

    def where(slot, step, filled, coords):
        held = filled[0, 0, 0]
        last = jnp.maximum(held - 1, 0)
        return (0, 0, 0, jnp.minimum(slot, last), jnp.where(slot < held, step, BLK // STEP - 1), 0, 0)

    f32, i16 = jnp.float32, jnp.int16
    outs = [jax.ShapeDtypeStruct((some_b, rank), f32), jax.ShapeDtypeStruct((some_a + some_c, rank), f32)]
    outs += [jax.ShapeDtypeStruct((some_b + PAD, rank), i16)] * (nx - 1)
    outs += [jax.ShapeDtypeStruct((some_a + some_c + PAD, rank), i16)] * (ny - 1)
    results = pl.pallas_call(
        functools.partial(block_kernel, nx, ny, nz),
        grid_spec=pltpu.PrefetchScalarGridSpec(
            num_scalar_prefetch=2,
            grid=(slots, BLK // STEP),
            in_specs=[
                pl.BlockSpec((1, 1, 1, 1, STEP, BLK, BLK), where),
                pl.BlockSpec((1, 1, 1, 1, STEP, BLK), lambda *at: where(*at)[:-1]),
                *map(whole, got_b),
                *map(whole, got_ac),
            ],
            out_specs=[*map(whole, outs)],
            scratch_shapes=[pltpu.VMEM((n, rank), jnp.bfloat16) for n in (all_a, all_b, all_c)]
            + [pltpu.VMEM((n, rank), f32) for n in (all_a, all_b, all_c)],
        ),
        out_shape=outs,
        compiler_params=pltpu.CompilerParams(
            vmem_limit_bytes=40 * 2**20, dimension_semantics=("arbitrary", "arbitrary")
        ),
        name="blocks",
    )(block_counts, block_coords, tensor_blocks, fiber_mask, *got_b, *got_ac)

    own_b, own_ac = results[:2]
    got_b = [shift(r, "gx", nx, i + 1) for i, r in enumerate(results[2 : 1 + nx])]
    got_ac = [shift(r, "gy", ny, i + 1) for i, r in enumerate(results[1 + nx :])]
    outs = [jax.ShapeDtypeStruct((per_b + per_a, rank), f32), jax.ShapeDtypeStruct((per_c, rank), f32)]
    outs += [jax.ShapeDtypeStruct((per_b + per_a + PAD, rank), i16)] * (nz - 1)
    outs += [jax.ShapeDtypeStruct((per_c + PAD, rank), i16)] * (nx - 1)
    results = pl.pallas_call(
        functools.partial(middle_kernel, nx, ny, nz, (some_b, some_c, some_a)),
        out_shape=outs,
        scratch_shapes=[pltpu.VMEM((n, rank), f32) for n in (some_b, some_c, some_a)],
        compiler_params=pltpu.CompilerParams(vmem_limit_bytes=32 * 2**20),
        name="middle",
    )(own_b, own_ac, *got_b, *got_ac)

    own_ba, own_c = results[:2]
    got_ba = [shift(r, "gz", nz, i + 1) for i, r in enumerate(results[2 : 1 + nz])]
    got_c = [shift(r, "gx", nx, i + 1) for i, r in enumerate(results[1 + nz :])]
    return pl.pallas_call(
        functools.partial(last_kernel, nx, nz, (per_b, per_c, per_a)),
        out_shape=[jax.ShapeDtypeStruct((1, n, rank), f32) for n in (per_a, per_b, per_c)],
        compiler_params=pltpu.CompilerParams(vmem_limit_bytes=32 * 2**20),
        name="last",
    )(own_ba, own_c, *got_ba, *got_c)


def solution(mesh):
    nx, ny, nz = (mesh.shape[name] for name in ("gx", "gy", "gz"))
    placed = (
        P("gx", "gy", "gz", None, None, None, None),
        P("gx", "gy", "gz", None, None, None),
        P("gx", "gy", "gz", None, None),
        P("gx", "gy", "gz"),
        P("gx", ("gy", "gz"), None),
        P("gy", ("gx", "gz"), None),
        P("gz", ("gx", "gy"), None),
    )
    return jax.shard_map(
        functools.partial(per_device, nx, ny, nz),
        mesh=mesh,
        in_specs=placed,
        out_specs=(
            P("gx", ("gy", "gz"), None),
            P("gy", ("gx", "gz"), None),
            P("gz", ("gx", "gy"), None),
        ),
        check_vma=False,
    )
```

```python
import functools

import jax
import jax.numpy as jnp
from jax import lax
from jax.experimental import pallas as pl
from jax.experimental.pallas import tpu as pltpu
from jax.sharding import PartitionSpec as P

BLK = 128
CHUNK = 32
GROUP = 8
PAD = 16
TOP = 32000.0


def pack(parts, target):
    at, powers = 0, []
    for part in parts:
        largest = jnp.maximum(jnp.max(jnp.abs(part), 0, keepdims=True), 1e-33)
        power = jnp.clip(jnp.ceil(jnp.log2(largest * (1.0 / TOP))), -120.0, 120.0)
        values = jnp.round(part * jnp.exp2(-power)).astype(jnp.int32)
        target[at : at + part.shape[0], :] = values.astype(jnp.int16)
        powers.append(power.astype(jnp.int32))
        at += part.shape[0]
    fill = jnp.zeros((PAD - len(powers), powers[0].shape[1]), jnp.int32)
    target[at : at + PAD, :] = jnp.concatenate([*powers, fill], 0).astype(jnp.int16)


def unpack(source, sizes):
    at, parts = 0, []
    powers = source[sum(sizes) : sum(sizes) + PAD, :].astype(jnp.int32).astype(jnp.float32)
    for i, size in enumerate(sizes):
        values = source[at : at + size, :].astype(jnp.int32).astype(jnp.float32)
        parts.append(values * jnp.exp2(powers[i : i + 1, :]))
        at += size
    return parts


def add_block(slot, coords, weights, slabs, grads, held):
    slab_a, slab_b, slab_c = slabs
    grad_a, grad_b, grad_c = grads
    f32, bf16 = jnp.float32, jnp.bfloat16
    at_a, at_b, at_c = (pl.multiple_of(coords[0, 0, 0, i, slot] * BLK, BLK) for i in range(3))
    rows_a = slab_a[pl.ds(at_a, BLK), :].astype(f32)
    rows_b = slab_b[pl.ds(at_b, BLK), :]
    rows_c = slab_c[pl.ds(at_c, BLK), :]
    rank = rows_b.shape[1]
    wide_b = rows_b.astype(f32)
    weight = weights[slot]

    def start(first):
        mixed = []
        for u in range(first, first + GROUP):
            row = jnp.broadcast_to(rows_a[u : u + 1, :], (16, rank)).astype(bf16)
            mixed.append((rows_b.reshape(BLK // 16, 16, rank) * row[None]).reshape(BLK, rank))
        mixed = jnp.concatenate(mixed, 0)
        return mixed, lax.dot_general(mixed, rows_c, (((1,), (1,)), ((), ())), preferred_element_type=f32)

    sum_b = sum_c = jnp.zeros((BLK, rank), f32)
    parts = []
    later = start(0)
    for first in range(0, BLK, GROUP):
        mixed, rate = later
        if first + GROUP < BLK:
            later = start(first + GROUP)
        error = []
        for i in range(GROUP):
            seen = held[slot, first + i].astype(f32)
            one = (jnp.exp(rate[i * BLK : (i + 1) * BLK]) - seen).astype(bf16)
            error.append(one * weight[:, first + i : first + i + 1])
        error = jnp.concatenate(error, 0)
        spread = jnp.dot(error, rows_c, preferred_element_type=f32)
        for i in range(GROUP):
            mine = spread[i * BLK : (i + 1) * BLK]
            sum_b = sum_b + mine * rows_a[first + i : first + i + 1, :]
            parts.append(jnp.sum(mine * wide_b, 0, keepdims=True))
        sum_c = sum_c + lax.dot_general(error, mixed, (((0,), (0,)), ((), ())), preferred_element_type=f32)
    grad_a[pl.ds(at_a, BLK), :] += jnp.concatenate(parts, 0)
    grad_b[pl.ds(at_b, BLK), :] += sum_b
    grad_c[pl.ds(at_c, BLK), :] += sum_c


def block_kernel(nx, ny, nz, filled, coords, entries, weights, *refs):
    got_b, got_ac = refs[:nx], refs[nx : nx + ny]
    refs = refs[nx + ny :]
    own_b, own_ac = refs[:2]
    send_b, send_ac = refs[2 : 1 + nx], refs[1 + nx : nx + ny]
    slab_a, slab_b, slab_c, grad_a, grad_b, grad_c, held, arrivals = refs[nx + ny :]
    x, y, z = (lax.axis_index(name) for name in ("gx", "gy", "gz"))
    all_a, all_b, all_c = (s.shape[0] for s in (slab_a, slab_b, slab_c))
    per_a, per_b, per_c = all_a // (ny * nz), all_b // (nx * nz), all_c // (nx * ny)
    count = filled[0, 0, 0]

    def copy(slot, chunk):
        rows = pl.ds(chunk * CHUNK, CHUNK)
        return pltpu.make_async_copy(
            entries.at[0, 0, 0, slot, rows], held.at[slot, rows], arrivals.at[slot, chunk]
        )

    def fetch(slot):
        @pl.when(slot < count)
        def _():
            for chunk in range(BLK // CHUNK):
                copy(slot, chunk).start()

    fetch(0)
    grad_a[...] = jnp.zeros_like(grad_a)
    grad_b[...] = jnp.zeros_like(grad_b)
    grad_c[...] = jnp.zeros_like(grad_c)
    for j in range(nz):
        of_z = lax.rem(z + nz - j, nz)
        for i in range(nx):
            at = (lax.rem(x + nx - i, nx) * nz + of_z) * per_b
            slab_b[pl.ds(pl.multiple_of(at, per_b), per_b), :] = got_b[i][j * per_b : (j + 1) * per_b, :]
        for i in range(ny):
            at = (lax.rem(y + ny - i, ny) * nz + of_z) * per_a
            slab_a[pl.ds(pl.multiple_of(at, per_a), per_a), :] = got_ac[i][j * per_a : (j + 1) * per_a, :]
    for j in range(nx):
        of_x = lax.rem(x + nx - j, nx)
        for i in range(ny):
            at = (of_x * ny + lax.rem(y + ny - i, ny)) * per_c
            first = nz * per_a + j * per_c
            slab_c[pl.ds(pl.multiple_of(at, per_c), per_c), :] = got_ac[i][first : first + per_c, :]

    @pl.loop(0, count)
    def _(slot):
        slabs, grads = (slab_a, slab_b, slab_c), (grad_a, grad_b, grad_c)
        for chunk in range(BLK // CHUNK):
            copy(slot, chunk).wait()
        fetch(slot + 1)
        add_block(slot, coords, weights, slabs, grads, held)

    some_b, some_a = all_b // nx, all_a // ny
    for i in range(nx):
        to_x = lax.rem(x + i, nx)
        part_b = grad_b[pl.ds(pl.multiple_of(to_x * some_b, some_b), some_b), :]
        if i == 0:
            own_b[...] = part_b
        else:
            pack((part_b,), send_b[i - 1])
    for i in range(ny):
        to_y = lax.rem(y + i, ny)
        part_a = grad_a[pl.ds(pl.multiple_of(to_y * some_a, some_a), some_a), :]
        part_c = jnp.concatenate(
            [grad_c[pl.ds(pl.multiple_of((j * ny + to_y) * per_c, per_c), per_c), :] for j in range(nx)], 0
        )
        if i == 0:
            own_ac[:some_a, :] = part_a
            own_ac[some_a:, :] = part_c
        else:
            pack((part_a, part_c), send_ac[i - 1])


def middle_kernel(nx, ny, nz, sizes, *refs):
    some_b, some_c, some_a = sizes
    own_b, own_ac = refs[:2]
    got_b, got_ac = refs[2 : 1 + nx], refs[1 + nx : nx + ny]
    own_ba, own_c = refs[nx + ny : nx + ny + 2]
    send_ba = refs[nx + ny + 2 : nx + ny + 1 + nz]
    send_c = refs[nx + ny + 1 + nz : 2 * nx + ny + nz]
    sum_b, sum_c, sum_a = refs[2 * nx + ny + nz :]
    x, z = lax.axis_index("gx"), lax.axis_index("gz")
    total_b, total_a, total_c = own_b[...], own_ac[:some_a, :], own_ac[some_a:, :]
    for ref in got_b:
        total_b = total_b + unpack(ref, (some_b,))[0]
    for ref in got_ac:
        part_a, part_c = unpack(ref, (some_a, some_c))
        total_a, total_c = total_a + part_a, total_c + part_c
    sum_b[...], sum_c[...], sum_a[...] = total_b, total_c, total_a
    per_b, per_c, per_a = some_b // nz, some_c // nx, some_a // nz
    for i in range(nz):
        to_z = lax.rem(z + i, nz)
        part_b = sum_b[pl.ds(pl.multiple_of(to_z * per_b, per_b), per_b), :]
        part_a = sum_a[pl.ds(pl.multiple_of(to_z * per_a, per_a), per_a), :]
        if i == 0:
            own_ba[:per_b, :] = part_b
            own_ba[per_b:, :] = part_a
        else:
            pack((part_b, part_a), send_ba[i - 1])
    for i in range(nx):
        to_x = lax.rem(x + i, nx)
        part_c = sum_c[pl.ds(pl.multiple_of(to_x * per_c, per_c), per_c), :]
        if i == 0:
            own_c[...] = part_c
        else:
            pack((part_c,), send_c[i - 1])


def last_kernel(nx, nz, sizes, *refs):
    per_b, per_c, per_a = sizes
    own_ba, own_c = refs[:2]
    got_ba, got_c = refs[2 : 1 + nz], refs[1 + nz : nz + nx]
    grad_a, grad_b, grad_c = refs[nz + nx :]
    total_b, total_a, total_c = own_ba[:per_b, :], own_ba[per_b:, :], own_c[...]
    for ref in got_ba:
        part_b, part_a = unpack(ref, (per_b, per_a))
        total_b, total_a = total_b + part_b, total_a + part_a
    for ref in got_c:
        total_c = total_c + unpack(ref, (per_c,))[0]
    grad_a[0] = total_a * (1.0 / BLK)
    grad_b[0] = total_b * (1.0 / BLK)
    grad_c[0] = total_c * (1.0 / BLK)


def shift(array, axis, size, by):
    return lax.ppermute(array, axis, [(i, (i + by) % size) for i in range(size)])


def around(array, axis, size):
    return [array] + [shift(array, axis, size, by) for by in range(1, size)]


def per_device(nx, ny, nz, tensor_blocks, fiber_mask, block_coords, block_counts, factor_a, factor_b, factor_c):
    per_a, per_b, per_c = (f.shape[1] for f in (factor_a, factor_b, factor_c))
    rank = factor_a.shape[2]
    all_a, all_b, all_c = per_a * ny * nz, per_b * nx * nz, per_c * nx * ny
    some_a, some_b, some_c = per_a * nz, per_b * nz, per_c * nx
    slots = tensor_blocks.shape[3]

    along_z = around(jnp.concatenate([factor_b[0], factor_a[0]], 0), "gz", nz)
    along_x = around(factor_c[0], "gx", nx)
    got_b = around(jnp.concatenate([p[:per_b] for p in along_z], 0), "gx", nx)
    got_ac = around(jnp.concatenate([p[per_b:] for p in along_z] + along_x, 0), "gy", ny)

    weights = jnp.swapaxes(fiber_mask[0, 0, 0], 1, 2).astype(jnp.bfloat16)
    f32, i16 = jnp.float32, jnp.int16
    outs = [jax.ShapeDtypeStruct((some_b, rank), f32), jax.ShapeDtypeStruct((some_a + some_c, rank), f32)]
    outs += [jax.ShapeDtypeStruct((some_b + PAD, rank), i16)] * (nx - 1)
    outs += [jax.ShapeDtypeStruct((some_a + some_c + PAD, rank), i16)] * (ny - 1)
    results = pl.pallas_call(
        functools.partial(block_kernel, nx, ny, nz),
        in_specs=[pl.BlockSpec(memory_space=pltpu.SMEM)] * 2
        + [pl.BlockSpec(memory_space=pl.ANY)]
        + [pl.BlockSpec(memory_space=pltpu.VMEM)] * (1 + nx + ny),
        scratch_shapes=[pltpu.VMEM((n, rank), jnp.bfloat16) for n in (all_a, all_b, all_c)]
        + [pltpu.VMEM((n, rank), f32) for n in (all_a, all_b, all_c)]
        + [pltpu.VMEM((slots, BLK, BLK, BLK), jnp.bfloat16), pltpu.SemaphoreType.DMA((slots, BLK // CHUNK))],
        out_shape=outs,
        compiler_params=pltpu.CompilerParams(vmem_limit_bytes=44 * 2**20),
        name="blocks",
    )(block_counts, block_coords, tensor_blocks, weights, *got_b, *got_ac)

    own_b, own_ac = results[:2]
    got_b = [shift(r, "gx", nx, i + 1) for i, r in enumerate(results[2 : 1 + nx])]
    got_ac = [shift(r, "gy", ny, i + 1) for i, r in enumerate(results[1 + nx :])]
    outs = [jax.ShapeDtypeStruct((per_b + per_a, rank), f32), jax.ShapeDtypeStruct((per_c, rank), f32)]
    outs += [jax.ShapeDtypeStruct((per_b + per_a + PAD, rank), i16)] * (nz - 1)
    outs += [jax.ShapeDtypeStruct((per_c + PAD, rank), i16)] * (nx - 1)
    results = pl.pallas_call(
        functools.partial(middle_kernel, nx, ny, nz, (some_b, some_c, some_a)),
        out_shape=outs,
        scratch_shapes=[pltpu.VMEM((n, rank), f32) for n in (some_b, some_c, some_a)],
        compiler_params=pltpu.CompilerParams(vmem_limit_bytes=32 * 2**20),
        name="middle",
    )(own_b, own_ac, *got_b, *got_ac)

    own_ba, own_c = results[:2]
    got_ba = [shift(r, "gz", nz, i + 1) for i, r in enumerate(results[2 : 1 + nz])]
    got_c = [shift(r, "gx", nx, i + 1) for i, r in enumerate(results[1 + nz :])]
    return pl.pallas_call(
        functools.partial(last_kernel, nx, nz, (per_b, per_c, per_a)),
        out_shape=[jax.ShapeDtypeStruct((1, n, rank), f32) for n in (per_a, per_b, per_c)],
        compiler_params=pltpu.CompilerParams(vmem_limit_bytes=32 * 2**20),
        name="last",
    )(own_ba, own_c, *got_ba, *got_c)


def solution(mesh):
    nx, ny, nz = (mesh.shape[name] for name in ("gx", "gy", "gz"))
    placed = (
        P("gx", "gy", "gz", None, None, None, None),
        P("gx", "gy", "gz", None, None, None),
        P("gx", "gy", "gz", None, None),
        P("gx", "gy", "gz"),
        P("gx", ("gy", "gz"), None),
        P("gy", ("gx", "gz"), None),
        P("gz", ("gx", "gy"), None),
    )
    return jax.shard_map(
        functools.partial(per_device, nx, ny, nz),
        mesh=mesh,
        in_specs=placed,
        out_specs=(
            P("gx", ("gy", "gz"), None),
            P("gy", ("gx", "gz"), None),
            P("gz", ("gx", "gy"), None),
        ),
        check_vma=False,
    )
```

```python
import functools

import jax
import jax.numpy as jnp
from jax import lax
from jax.experimental import pallas as pl
from jax.experimental.pallas import tpu as pltpu
from jax.sharding import PartitionSpec as P

BLK = 128
CHUNK = 32
GROUP = 8
PAD = 16
TOP = 32000.0


def pack(parts, target):
    at, powers = 0, []
    for part in parts:
        largest = jnp.maximum(jnp.max(jnp.abs(part), 0, keepdims=True), 1e-33)
        power = jnp.clip(jnp.ceil(jnp.log2(largest * (1.0 / TOP))), -120.0, 120.0)
        values = jnp.round(part * jnp.exp2(-power)).astype(jnp.int32)
        target[at : at + part.shape[0], :] = values.astype(jnp.int16)
        powers.append(power.astype(jnp.int32))
        at += part.shape[0]
    fill = jnp.zeros((PAD - len(powers), powers[0].shape[1]), jnp.int32)
    target[at : at + PAD, :] = jnp.concatenate([*powers, fill], 0).astype(jnp.int16)


def unpack(source, sizes):
    at, parts = 0, []
    powers = source[sum(sizes) : sum(sizes) + PAD, :].astype(jnp.int32).astype(jnp.float32)
    for i, size in enumerate(sizes):
        values = source[at : at + size, :].astype(jnp.int32).astype(jnp.float32)
        parts.append(values * jnp.exp2(powers[i : i + 1, :]))
        at += size
    return parts


def take(items, *counts):
    runs = []
    for count in counts:
        runs.append(items[:count])
        items = items[count:]
    return runs


def add_block(slot, places, weights, slabs, grads, held):
    slab_a, slab_b, slab_c = slabs
    grad_a, grad_b, grad_c = grads
    f32, bf16 = jnp.float32, jnp.bfloat16
    at_a, at_b, at_c = (pl.multiple_of(places[i] * BLK, BLK) for i in range(3))
    rows_a = slab_a[pl.ds(at_a, BLK), :].astype(f32)
    rows_b = slab_b[pl.ds(at_b, BLK), :]
    rows_c = slab_c[pl.ds(at_c, BLK), :]
    rank = rows_b.shape[1]
    wide_b = rows_b.astype(f32)
    weight = jnp.transpose(weights[slot].astype(f32)).astype(bf16)

    def start(first):
        mixed = []
        for u in range(first, first + GROUP):
            row = jnp.broadcast_to(rows_a[u : u + 1, :], (16, rank)).astype(bf16)
            mixed.append((rows_b.reshape(BLK // 16, 16, rank) * row[None]).reshape(BLK, rank))
        mixed = jnp.concatenate(mixed, 0)
        return mixed, lax.dot_general(mixed, rows_c, (((1,), (1,)), ((), ())), preferred_element_type=f32)

    sum_b = sum_c = jnp.zeros((BLK, rank), f32)
    parts = []
    later = start(0)
    for first in range(0, BLK, GROUP):
        mixed, rate = later
        if first + GROUP < BLK:
            later = start(first + GROUP)
        error = []
        for i in range(GROUP):
            seen = held[slot, first + i].astype(f32)
            one = (jnp.exp(rate[i * BLK : (i + 1) * BLK]) - seen).astype(bf16)
            error.append(one * weight[:, first + i : first + i + 1])
        error = jnp.concatenate(error, 0)
        spread = jnp.dot(error, rows_c, preferred_element_type=f32)
        for i in range(GROUP):
            mine = spread[i * BLK : (i + 1) * BLK]
            sum_b = sum_b + mine * rows_a[first + i : first + i + 1, :]
            parts.append(jnp.sum(mine * wide_b, 0, keepdims=True))
        sum_c = sum_c + lax.dot_general(error, mixed, (((0,), (0,)), ((), ())), preferred_element_type=f32)
    grad_a[pl.ds(at_a, BLK), :] += jnp.concatenate(parts, 0)
    grad_b[pl.ds(at_b, BLK), :] += sum_b
    grad_c[pl.ds(at_c, BLK), :] += sum_c


def block_kernel(nx, ny, nz, table, entries, weights, *refs):
    along_z, along_x, rest_b, got_ac = take(refs, nz, nx, nx - 1, ny)
    refs = refs[nz + 2 * nx - 1 + ny :]
    own_b, own_ac = refs[:2]
    send_b, send_ac = refs[2 : 1 + nx], refs[1 + nx : nx + ny]
    slab_a, slab_b, slab_c, grad_a, grad_b, grad_c, held, arrivals = refs[nx + ny :]
    x, y, z = (lax.axis_index(name) for name in ("gx", "gy", "gz"))
    all_a, all_b, all_c = (s.shape[0] for s in (slab_a, slab_b, slab_c))
    per_a, per_b, per_c = all_a // (ny * nz), all_b // (nx * nz), all_c // (nx * ny)
    count = table[0]

    def copy(slot, chunk):
        rows = pl.ds(chunk * CHUNK, CHUNK)
        return pltpu.make_async_copy(
            entries.at[0, 0, 0, slot, rows], held.at[slot, rows], arrivals.at[slot, chunk]
        )

    def fetch(slot):
        @pl.when(slot < count)
        def _():
            for chunk in range(BLK // CHUNK):
                copy(slot, chunk).start()

    fetch(0)
    grad_a[...] = jnp.zeros_like(grad_a)
    grad_b[...] = jnp.zeros_like(grad_b)
    grad_c[...] = jnp.zeros_like(grad_c)
    for j in range(nz):
        of_z = lax.rem(z + nz - j, nz)
        for i in range(nx):
            at = (lax.rem(x + nx - i, nx) * nz + of_z) * per_b
            if i == 0:
                rows = along_z[j][:per_b, :]
            elif j == 0:
                rows = along_x[i][per_c:, :]
            else:
                rows = rest_b[i - 1][(j - 1) * per_b : j * per_b, :]
            slab_b[pl.ds(pl.multiple_of(at, per_b), per_b), :] = rows
        for i in range(ny):
            at = (before(y, i, ny) * nz + of_z) * per_a
            slab_a[pl.ds(pl.multiple_of(at, per_a), per_a), :] = got_ac[i][j * per_a : (j + 1) * per_a, :]
    for j in range(nx):
        of_x = lax.rem(x + nx - j, nx)
        for i in range(ny):
            at = (of_x * ny + before(y, i, ny)) * per_c
            first = nz * per_a + j * per_c
            slab_c[pl.ds(pl.multiple_of(at, per_c), per_c), :] = got_ac[i][first : first + per_c, :]

    @pl.loop(0, count)
    def _(slot):
        slabs, grads = (slab_a, slab_b, slab_c), (grad_a, grad_b, grad_c)
        for chunk in range(BLK // CHUNK):
            copy(slot, chunk).wait()
        fetch(slot + 1)
        places = [table[1 + 3 * slot + i] for i in range(3)]
        add_block(slot, places, weights, slabs, grads, held)

    some_b, some_a = all_b // nx, all_a // ny
    for i in range(nx):
        to_x = lax.rem(x + i, nx)
        part_b = grad_b[pl.ds(pl.multiple_of(to_x * some_b, some_b), some_b), :]
        if i == 0:
            own_b[...] = part_b
        else:
            pack((part_b,), send_b[i - 1])
    for i in range(ny):
        to_y = lax.rem(y + i, ny)
        part_a = grad_a[pl.ds(pl.multiple_of(to_y * some_a, some_a), some_a), :]
        part_c = jnp.concatenate(
            [grad_c[pl.ds(pl.multiple_of((j * ny + to_y) * per_c, per_c), per_c), :] for j in range(nx)], 0
        )
        if i == 0:
            own_ac[:some_a, :] = part_a
            own_ac[some_a:, :] = part_c
        else:
            pack((part_a, part_c), send_ac[i - 1])


def middle_kernel(nx, ny, nz, sizes, *refs):
    some_b, some_c, some_a = sizes
    own_b, own_ac = refs[:2]
    got_b, got_ac = refs[2 : 1 + nx], refs[1 + nx : nx + ny]
    own_ba, own_c = refs[nx + ny : nx + ny + 2]
    send_ba = refs[nx + ny + 2 : nx + ny + 1 + nz]
    send_c = refs[nx + ny + 1 + nz : 2 * nx + ny + nz]
    sum_b, sum_c, sum_a = refs[2 * nx + ny + nz :]
    x, z = lax.axis_index("gx"), lax.axis_index("gz")
    total_b, total_a, total_c = own_b[...], own_ac[:some_a, :], own_ac[some_a:, :]
    for ref in got_b:
        total_b = total_b + unpack(ref, (some_b,))[0]
    for ref in got_ac:
        part_a, part_c = unpack(ref, (some_a, some_c))
        total_a, total_c = total_a + part_a, total_c + part_c
    sum_b[...], sum_c[...], sum_a[...] = total_b, total_c, total_a
    per_b, per_c, per_a = some_b // nz, some_c // nx, some_a // nz
    for i in range(nz):
        to_z = lax.rem(z + i, nz)
        part_b = sum_b[pl.ds(pl.multiple_of(to_z * per_b, per_b), per_b), :]
        part_a = sum_a[pl.ds(pl.multiple_of(to_z * per_a, per_a), per_a), :]
        if i == 0:
            own_ba[:per_b, :] = part_b
            own_ba[per_b:, :] = part_a
        else:
            pack((part_b, part_a), send_ba[i - 1])
    for i in range(nx):
        to_x = lax.rem(x + i, nx)
        part_c = sum_c[pl.ds(pl.multiple_of(to_x * per_c, per_c), per_c), :]
        if i == 0:
            own_c[...] = part_c
        else:
            pack((part_c,), send_c[i - 1])


def last_kernel(nx, nz, sizes, *refs):
    per_b, per_c, per_a = sizes
    own_ba, own_c = refs[:2]
    got_ba, got_c = refs[2 : 1 + nz], refs[1 + nz : nz + nx]
    grad_a, grad_b, grad_c = refs[nz + nx :]
    total_b, total_a, total_c = own_ba[:per_b, :], own_ba[per_b:, :], own_c[...]
    for ref in got_ba:
        part_b, part_a = unpack(ref, (per_b, per_a))
        total_b, total_a = total_b + part_b, total_a + part_a
    for ref in got_c:
        total_c = total_c + unpack(ref, (per_c,))[0]
    grad_a[0] = total_a * (1.0 / BLK)
    grad_b[0] = total_b * (1.0 / BLK)
    grad_c[0] = total_c * (1.0 / BLK)


def shift(array, axis, size, by):
    return lax.ppermute(array, axis, [(i, (i + by) % size) for i in range(size)])


def around(array, axis, size):
    return [array] + [shift(array, axis, size, by) for by in range(1, size)]


def pairwise(array, axis, size):
    near = 2 - size % 2
    far = [array] + [shift(array, axis, size, by) for by in range(near, size, near)]
    if near == 1:
        return far
    swapped = [lax.ppermute(item, axis, [(i, i ^ 1) for i in range(size)]) for item in far]
    return [item for pair in zip(far, swapped) for item in pair]


def before(me, place, size):
    near = 2 - size % 2
    if place % near:
        me = me + 1 - 2 * lax.rem(me, 2)
    return lax.rem(me + size - place // near * near, size)


def per_device(nx, ny, nz, tensor_blocks, fiber_mask, block_coords, block_counts, factor_a, factor_b, factor_c):
    per_a, per_b, per_c = (f.shape[1] for f in (factor_a, factor_b, factor_c))
    rank = factor_a.shape[2]
    all_a, all_b, all_c = per_a * ny * nz, per_b * nx * nz, per_c * nx * ny
    some_a, some_b, some_c = per_a * nz, per_b * nz, per_c * nx
    slots = tensor_blocks.shape[3]

    along_z = around(jnp.concatenate([factor_b[0], factor_a[0]], 0), "gz", nz)
    weights = fiber_mask[0, 0, 0].astype(jnp.bfloat16)
    table = jnp.concatenate([block_counts.reshape(1), jnp.swapaxes(block_coords[0, 0, 0], 0, 1).reshape(3 * slots)])
    rows_cb = jnp.concatenate([factor_c[0], factor_b[0]], 0)
    rows_cb, weights, table = lax.optimization_barrier((rows_cb, weights, table))
    along_x = around(rows_cb, "gx", nx)
    some_ac = jnp.concatenate([p[per_b:] for p in along_z] + [p[:per_c] for p in along_x], 0)
    got_ac = pairwise(some_ac, "gy", ny)
    rest_b = around(jnp.concatenate([p[:per_b] for p in along_z[1:]], 0), "gx", nx)[1:]
    f32, i16 = jnp.float32, jnp.int16
    outs = [jax.ShapeDtypeStruct((some_b, rank), f32), jax.ShapeDtypeStruct((some_a + some_c, rank), f32)]
    outs += [jax.ShapeDtypeStruct((some_b + PAD, rank), i16)] * (nx - 1)
    outs += [jax.ShapeDtypeStruct((some_a + some_c + PAD, rank), i16)] * (ny - 1)
    results = pl.pallas_call(
        functools.partial(block_kernel, nx, ny, nz),
        in_specs=[pl.BlockSpec(memory_space=pltpu.SMEM), pl.BlockSpec(memory_space=pl.ANY)]
        + [pl.BlockSpec(memory_space=pltpu.VMEM)] * (nz + 2 * nx + ny),
        scratch_shapes=[pltpu.VMEM((n, rank), jnp.bfloat16) for n in (all_a, all_b, all_c)]
        + [pltpu.VMEM((n, rank), f32) for n in (all_a, all_b, all_c)]
        + [pltpu.VMEM((slots, BLK, BLK, BLK), jnp.bfloat16), pltpu.SemaphoreType.DMA((slots, BLK // CHUNK))],
        out_shape=outs,
        compiler_params=pltpu.CompilerParams(vmem_limit_bytes=44 * 2**20),
        name="blocks",
    )(table, tensor_blocks, weights, *along_z, *along_x, *rest_b, *got_ac)

    own_b, own_ac = results[:2]
    got_b = [shift(r, "gx", nx, i + 1) for i, r in enumerate(results[2 : 1 + nx])]
    got_ac = [shift(r, "gy", ny, i + 1) for i, r in enumerate(results[1 + nx :])]
    outs = [jax.ShapeDtypeStruct((per_b + per_a, rank), f32), jax.ShapeDtypeStruct((per_c, rank), f32)]
    outs += [jax.ShapeDtypeStruct((per_b + per_a + PAD, rank), i16)] * (nz - 1)
    outs += [jax.ShapeDtypeStruct((per_c + PAD, rank), i16)] * (nx - 1)
    results = pl.pallas_call(
        functools.partial(middle_kernel, nx, ny, nz, (some_b, some_c, some_a)),
        out_shape=outs,
        scratch_shapes=[pltpu.VMEM((n, rank), f32) for n in (some_b, some_c, some_a)],
        compiler_params=pltpu.CompilerParams(vmem_limit_bytes=32 * 2**20),
        name="middle",
    )(own_b, own_ac, *got_b, *got_ac)

    own_ba, own_c = results[:2]
    got_ba = [shift(r, "gz", nz, i + 1) for i, r in enumerate(results[2 : 1 + nz])]
    got_c = [shift(r, "gx", nx, i + 1) for i, r in enumerate(results[1 + nz :])]
    return pl.pallas_call(
        functools.partial(last_kernel, nx, nz, (per_b, per_c, per_a)),
        out_shape=[jax.ShapeDtypeStruct((1, n, rank), f32) for n in (per_a, per_b, per_c)],
        compiler_params=pltpu.CompilerParams(vmem_limit_bytes=32 * 2**20),
        name="last",
    )(own_ba, own_c, *got_ba, *got_c)


def solution(mesh):
    nx, ny, nz = (mesh.shape[name] for name in ("gx", "gy", "gz"))
    placed = (
        P("gx", "gy", "gz", None, None, None, None),
        P("gx", "gy", "gz", None, None, None),
        P("gx", "gy", "gz", None, None),
        P("gx", "gy", "gz"),
        P("gx", ("gy", "gz"), None),
        P("gy", ("gx", "gz"), None),
        P("gz", ("gx", "gy"), None),
    )
    return jax.shard_map(
        functools.partial(per_device, nx, ny, nz),
        mesh=mesh,
        in_specs=placed,
        out_specs=(
            P("gx", ("gy", "gz"), None),
            P("gy", ("gx", "gz"), None),
            P("gz", ("gx", "gy"), None),
        ),
        check_vma=False,
    )
```

```python
import functools

import jax
import jax.numpy as jnp
from jax import lax
from jax.experimental import pallas as pl
from jax.experimental.pallas import tpu as pltpu
from jax.sharding import PartitionSpec as P

BLK = 128
CHUNK = 32
GROUP = 8
PAD = 16
TOP = 32000.0


def pack(parts, target):
    at, powers = 0, []
    for part in parts:
        largest = jnp.maximum(jnp.max(jnp.abs(part), 0, keepdims=True), 1e-33)
        power = jnp.clip(jnp.ceil(jnp.log2(largest * (1.0 / TOP))), -120.0, 120.0)
        values = jnp.round(part * jnp.exp2(-power)).astype(jnp.int32)
        target[at : at + part.shape[0], :] = values.astype(jnp.int16)
        powers.append(power.astype(jnp.int32))
        at += part.shape[0]
    fill = jnp.zeros((PAD - len(powers), powers[0].shape[1]), jnp.int32)
    target[at : at + PAD, :] = jnp.concatenate([*powers, fill], 0).astype(jnp.int16)


def unpack(source, sizes):
    at, parts = 0, []
    powers = source[sum(sizes) : sum(sizes) + PAD, :].astype(jnp.int32).astype(jnp.float32)
    for i, size in enumerate(sizes):
        values = source[at : at + size, :].astype(jnp.int32).astype(jnp.float32)
        parts.append(values * jnp.exp2(powers[i : i + 1, :]))
        at += size
    return parts


def take(items, *counts):
    runs = []
    for count in counts:
        runs.append(items[:count])
        items = items[count:]
    return runs


def add_block(slot, places, weights, slabs, grads, held):
    slab_a, slab_b, slab_c = slabs
    grad_a, grad_b, grad_c = grads
    f32, bf16 = jnp.float32, jnp.bfloat16
    at_a, at_b, at_c = (pl.multiple_of(places[i] * BLK, BLK) for i in range(3))
    rows_a = slab_a[pl.ds(at_a, BLK), :].astype(f32)
    rows_b = slab_b[pl.ds(at_b, BLK), :]
    rows_c = slab_c[pl.ds(at_c, BLK), :]
    rank = rows_b.shape[1]
    wide_b = rows_b.astype(f32)
    weight = jnp.transpose(weights[slot].astype(f32)).astype(bf16)

    def start(first):
        mixed = []
        for u in range(first, first + GROUP):
            row = jnp.broadcast_to(rows_a[u : u + 1, :], (16, rank)).astype(bf16)
            mixed.append((rows_b.reshape(BLK // 16, 16, rank) * row[None]).reshape(BLK, rank))
        mixed = jnp.concatenate(mixed, 0)
        return mixed, lax.dot_general(mixed, rows_c, (((1,), (1,)), ((), ())), preferred_element_type=f32)

    sum_b = sum_c = jnp.zeros((BLK, rank), f32)
    parts = []
    later = start(0)
    for first in range(0, BLK, GROUP):
        mixed, rate = later
        if first + GROUP < BLK:
            later = start(first + GROUP)
        error = []
        for i in range(GROUP):
            seen = held[slot, first + i].astype(f32)
            one = (jnp.exp(rate[i * BLK : (i + 1) * BLK]) - seen).astype(bf16)
            error.append(one * weight[:, first + i : first + i + 1])
        error = jnp.concatenate(error, 0)
        spread = jnp.dot(error, rows_c, preferred_element_type=f32)
        for i in range(GROUP):
            mine = spread[i * BLK : (i + 1) * BLK]
            sum_b = sum_b + mine * rows_a[first + i : first + i + 1, :]
            parts.append(jnp.sum(mine * wide_b, 0, keepdims=True))
        sum_c = sum_c + lax.dot_general(error, mixed, (((0,), (0,)), ((), ())), preferred_element_type=f32)
    grad_a[pl.ds(at_a, BLK), :] += jnp.concatenate(parts, 0)
    grad_b[pl.ds(at_b, BLK), :] += sum_b
    grad_c[pl.ds(at_c, BLK), :] += sum_c


def block_kernel(nx, ny, nz, table, entries, weights, *refs):
    along_z, along_x, rest_b, got_ac = take(refs, nz, nx, nx - 1, ny)
    refs = refs[nz + 2 * nx - 1 + ny :]
    own_b, own_ac = refs[:2]
    send_b, send_ac = refs[2 : 1 + nx], refs[1 + nx : nx + ny]
    slab_a, slab_b, slab_c, grad_a, grad_b, grad_c, held, arrivals = refs[nx + ny :]
    x, y, z = (lax.axis_index(name) for name in ("gx", "gy", "gz"))
    all_a, all_b, all_c = (s.shape[0] for s in (slab_a, slab_b, slab_c))
    per_a, per_b, per_c = all_a // (ny * nz), all_b // (nx * nz), all_c // (nx * ny)
    count = table[0]

    def copy(slot, chunk):
        rows = pl.ds(chunk * CHUNK, CHUNK)
        return pltpu.make_async_copy(
            entries.at[0, 0, 0, slot, rows], held.at[slot, rows], arrivals.at[slot, chunk]
        )

    def fetch(slot):
        @pl.when(slot < count)
        def _():
            for chunk in range(BLK // CHUNK):
                copy(slot, chunk).start()

    fetch(0)
    grad_a[...] = jnp.zeros_like(grad_a)
    grad_b[...] = jnp.zeros_like(grad_b)
    grad_c[...] = jnp.zeros_like(grad_c)
    for j in range(nz):
        of_z = lax.rem(z + nz - j, nz)
        for i in range(nx):
            at = (lax.rem(x + nx - i, nx) * nz + of_z) * per_b
            if i == 0:
                rows = along_z[j][:per_b, :]
            elif j == 0:
                rows = along_x[i][per_c:, :]
            else:
                rows = rest_b[i - 1][(j - 1) * per_b : j * per_b, :]
            slab_b[pl.ds(pl.multiple_of(at, per_b), per_b), :] = rows
        for i in range(ny):
            at = (before(y, i, ny) * nz + of_z) * per_a
            slab_a[pl.ds(pl.multiple_of(at, per_a), per_a), :] = got_ac[i][j * per_a : (j + 1) * per_a, :]
    for j in range(nx):
        of_x = lax.rem(x + nx - j, nx)
        for i in range(ny):
            at = (of_x * ny + before(y, i, ny)) * per_c
            first = nz * per_a + j * per_c
            slab_c[pl.ds(pl.multiple_of(at, per_c), per_c), :] = got_ac[i][first : first + per_c, :]

    @pl.loop(0, count)
    def _(slot):
        slabs, grads = (slab_a, slab_b, slab_c), (grad_a, grad_b, grad_c)
        for chunk in range(BLK // CHUNK):
            copy(slot, chunk).wait()
        fetch(slot + 1)
        places = [table[1 + 3 * slot + i] for i in range(3)]
        add_block(slot, places, weights, slabs, grads, held)

    some_b, some_a = all_b // nx, all_a // ny
    for i in range(nx):
        to_x = lax.rem(x + i, nx)
        part_b = grad_b[pl.ds(pl.multiple_of(to_x * some_b, some_b), some_b), :]
        if i == 0:
            own_b[...] = part_b
        else:
            pack((part_b,), send_b[i - 1])
    for i in range(ny):
        to_y = lax.rem(y + i, ny)
        part_a = grad_a[pl.ds(pl.multiple_of(to_y * some_a, some_a), some_a), :]
        part_c = jnp.concatenate(
            [grad_c[pl.ds(pl.multiple_of((j * ny + to_y) * per_c, per_c), per_c), :] for j in range(nx)], 0
        )
        if i == 0:
            own_ac[:some_a, :] = part_a
            own_ac[some_a:, :] = part_c
        else:
            pack((part_a, part_c), send_ac[i - 1])


def middle_kernel(nx, ny, nz, sizes, *refs):
    some_b, some_c, some_a = sizes
    own_b, own_ac = refs[:2]
    got_b, got_ac = refs[2 : 1 + nx], refs[1 + nx : nx + ny]
    own_ba, own_c = refs[nx + ny : nx + ny + 2]
    send_ba = refs[nx + ny + 2 : nx + ny + 1 + nz]
    send_c = refs[nx + ny + 1 + nz : 2 * nx + ny + nz]
    sum_b, sum_c, sum_a = refs[2 * nx + ny + nz :]
    x, z = lax.axis_index("gx"), lax.axis_index("gz")
    total_b, total_a, total_c = own_b[...], own_ac[:some_a, :], own_ac[some_a:, :]
    for ref in got_b:
        total_b = total_b + unpack(ref, (some_b,))[0]
    for ref in got_ac:
        part_a, part_c = unpack(ref, (some_a, some_c))
        total_a, total_c = total_a + part_a, total_c + part_c
    sum_b[...], sum_c[...], sum_a[...] = total_b, total_c, total_a
    per_b, per_c, per_a = some_b // nz, some_c // nx, some_a // nz
    for i in range(nz):
        to_z = lax.rem(z + i, nz)
        part_b = sum_b[pl.ds(pl.multiple_of(to_z * per_b, per_b), per_b), :]
        part_a = sum_a[pl.ds(pl.multiple_of(to_z * per_a, per_a), per_a), :]
        if i == 0:
            own_ba[:per_b, :] = part_b
            own_ba[per_b:, :] = part_a
        else:
            pack((part_b, part_a), send_ba[i - 1])
    for i in range(nx):
        to_x = lax.rem(x + i, nx)
        part_c = sum_c[pl.ds(pl.multiple_of(to_x * per_c, per_c), per_c), :]
        if i == 0:
            own_c[...] = part_c
        else:
            pack((part_c,), send_c[i - 1])


def last_kernel(nx, nz, sizes, *refs):
    per_b, per_c, per_a = sizes
    own_ba, own_c = refs[:2]
    got_ba, got_c = refs[2 : 1 + nz], refs[1 + nz : nz + nx]
    grad_a, grad_b, grad_c = refs[nz + nx :]
    total_b, total_a, total_c = own_ba[:per_b, :], own_ba[per_b:, :], own_c[...]
    for ref in got_ba:
        part_b, part_a = unpack(ref, (per_b, per_a))
        total_b, total_a = total_b + part_b, total_a + part_a
    for ref in got_c:
        total_c = total_c + unpack(ref, (per_c,))[0]
    grad_a[0] = total_a * (1.0 / BLK)
    grad_b[0] = total_b * (1.0 / BLK)
    grad_c[0] = total_c * (1.0 / BLK)


def shift(array, axis, size, by):
    return lax.ppermute(array, axis, [(i, (i + by) % size) for i in range(size)])


def around(array, axis, size):
    return [array] + [shift(array, axis, size, by) for by in range(1, size)]


def pairwise(array, axis, size):
    near = 2 - size % 2
    far = [array] + [shift(array, axis, size, by) for by in range(near, size, near)]
    if near == 1:
        return far
    swapped = [lax.ppermute(item, axis, [(i, i ^ 1) for i in range(size)]) for item in far]
    return [item for pair in zip(far, swapped) for item in pair]


def before(me, place, size):
    near = 2 - size % 2
    if place % near:
        me = me + 1 - 2 * lax.rem(me, 2)
    return lax.rem(me + size - place // near * near, size)


def per_device(nx, ny, nz, tensor_blocks, fiber_mask, block_coords, block_counts, factor_a, factor_b, factor_c):
    per_a, per_b, per_c = (f.shape[1] for f in (factor_a, factor_b, factor_c))
    rank = factor_a.shape[2]
    all_a, all_b, all_c = per_a * ny * nz, per_b * nx * nz, per_c * nx * ny
    some_a, some_b, some_c = per_a * nz, per_b * nz, per_c * nx
    slots = tensor_blocks.shape[3]

    along_z = around(jnp.concatenate([factor_b[0], factor_a[0]], 0), "gz", nz)
    weights = fiber_mask[0, 0, 0].astype(jnp.bfloat16)
    table = jnp.concatenate([block_counts.reshape(1), jnp.swapaxes(block_coords[0, 0, 0], 0, 1).reshape(3 * slots)])
    along_x = around(jnp.concatenate([factor_c[0], factor_b[0]], 0), "gx", nx)
    *along_z, weights, table = lax.optimization_barrier((*along_z, weights, table))
    some_ac = jnp.concatenate([p[per_b:] for p in along_z] + [p[:per_c] for p in along_x], 0)
    got_ac = pairwise(some_ac, "gy", ny)
    rest_b = around(jnp.concatenate([p[:per_b] for p in along_z[1:]], 0), "gx", nx)[1:]
    f32, i16 = jnp.float32, jnp.int16
    outs = [jax.ShapeDtypeStruct((some_b, rank), f32), jax.ShapeDtypeStruct((some_a + some_c, rank), f32)]
    outs += [jax.ShapeDtypeStruct((some_b + PAD, rank), i16)] * (nx - 1)
    outs += [jax.ShapeDtypeStruct((some_a + some_c + PAD, rank), i16)] * (ny - 1)
    results = pl.pallas_call(
        functools.partial(block_kernel, nx, ny, nz),
        in_specs=[pl.BlockSpec(memory_space=pltpu.SMEM), pl.BlockSpec(memory_space=pl.ANY)]
        + [pl.BlockSpec(memory_space=pltpu.VMEM)] * (nz + 2 * nx + ny),
        scratch_shapes=[pltpu.VMEM((n, rank), jnp.bfloat16) for n in (all_a, all_b, all_c)]
        + [pltpu.VMEM((n, rank), f32) for n in (all_a, all_b, all_c)]
        + [pltpu.VMEM((slots, BLK, BLK, BLK), jnp.bfloat16), pltpu.SemaphoreType.DMA((slots, BLK // CHUNK))],
        out_shape=outs,
        compiler_params=pltpu.CompilerParams(vmem_limit_bytes=44 * 2**20),
        name="blocks",
    )(table, tensor_blocks, weights, *along_z, *along_x, *rest_b, *got_ac)

    own_b, own_ac = results[:2]
    got_b = [shift(r, "gx", nx, i + 1) for i, r in enumerate(results[2 : 1 + nx])]
    got_ac = [shift(r, "gy", ny, i + 1) for i, r in enumerate(results[1 + nx :])]
    outs = [jax.ShapeDtypeStruct((per_b + per_a, rank), f32), jax.ShapeDtypeStruct((per_c, rank), f32)]
    outs += [jax.ShapeDtypeStruct((per_b + per_a + PAD, rank), i16)] * (nz - 1)
    outs += [jax.ShapeDtypeStruct((per_c + PAD, rank), i16)] * (nx - 1)
    results = pl.pallas_call(
        functools.partial(middle_kernel, nx, ny, nz, (some_b, some_c, some_a)),
        out_shape=outs,
        scratch_shapes=[pltpu.VMEM((n, rank), f32) for n in (some_b, some_c, some_a)],
        compiler_params=pltpu.CompilerParams(vmem_limit_bytes=32 * 2**20),
        name="middle",
    )(own_b, own_ac, *got_b, *got_ac)

    own_ba, own_c = results[:2]
    got_ba = [shift(r, "gz", nz, i + 1) for i, r in enumerate(results[2 : 1 + nz])]
    got_c = [shift(r, "gx", nx, i + 1) for i, r in enumerate(results[1 + nz :])]
    return pl.pallas_call(
        functools.partial(last_kernel, nx, nz, (per_b, per_c, per_a)),
        out_shape=[jax.ShapeDtypeStruct((1, n, rank), f32) for n in (per_a, per_b, per_c)],
        compiler_params=pltpu.CompilerParams(vmem_limit_bytes=32 * 2**20),
        name="last",
    )(own_ba, own_c, *got_ba, *got_c)


def solution(mesh):
    nx, ny, nz = (mesh.shape[name] for name in ("gx", "gy", "gz"))
    placed = (
        P("gx", "gy", "gz", None, None, None, None),
        P("gx", "gy", "gz", None, None, None),
        P("gx", "gy", "gz", None, None),
        P("gx", "gy", "gz"),
        P("gx", ("gy", "gz"), None),
        P("gy", ("gx", "gz"), None),
        P("gz", ("gx", "gy"), None),
    )
    return jax.shard_map(
        functools.partial(per_device, nx, ny, nz),
        mesh=mesh,
        in_specs=placed,
        out_specs=(
            P("gx", ("gy", "gz"), None),
            P("gy", ("gx", "gz"), None),
            P("gz", ("gx", "gy"), None),
        ),
        check_vma=False,
    )
```

```python
import functools

import jax
import jax.numpy as jnp
from jax import lax
from jax.experimental import pallas as pl
from jax.experimental.pallas import tpu as pltpu
from jax.sharding import PartitionSpec as P

BLK = 128
CHUNK = 32
GROUP = 8
PAD = 16
TOP = 32000.0


def pack(parts, target):
    at, powers = 0, []
    for part in parts:
        largest = jnp.maximum(jnp.max(jnp.abs(part), 0, keepdims=True), 1e-33)
        power = jnp.clip(jnp.ceil(jnp.log2(largest * (1.0 / TOP))), -120.0, 120.0)
        values = jnp.round(part * jnp.exp2(-power)).astype(jnp.int32)
        target[at : at + part.shape[0], :] = values.astype(jnp.int16)
        powers.append(power.astype(jnp.int32))
        at += part.shape[0]
    fill = jnp.zeros((PAD - len(powers), powers[0].shape[1]), jnp.int32)
    target[at : at + PAD, :] = jnp.concatenate([*powers, fill], 0).astype(jnp.int16)


def unpack(source, sizes):
    at, parts = 0, []
    powers = source[sum(sizes) : sum(sizes) + PAD, :].astype(jnp.int32).astype(jnp.float32)
    for i, size in enumerate(sizes):
        values = source[at : at + size, :].astype(jnp.int32).astype(jnp.float32)
        parts.append(values * jnp.exp2(powers[i : i + 1, :]))
        at += size
    return parts


def take(items, *counts):
    runs = []
    for count in counts:
        runs.append(items[:count])
        items = items[count:]
    return runs


def add_block(places, weight, slabs, grads, held):
    slab_a, slab_b, slab_c = slabs
    grad_a, grad_b, grad_c = grads
    f32, bf16 = jnp.float32, jnp.bfloat16
    at_a, at_b, at_c = (pl.multiple_of(places[i] * BLK, BLK) for i in range(3))
    rows_a = slab_a[pl.ds(at_a, BLK), :].astype(f32)
    rows_b = slab_b[pl.ds(at_b, BLK), :]
    rows_c = slab_c[pl.ds(at_c, BLK), :]
    rank = rows_b.shape[1]
    wide_b = rows_b.astype(f32)
    weight = jnp.transpose(weight.astype(f32)).astype(bf16)

    def start(first):
        mixed = []
        for u in range(first, first + GROUP):
            row = jnp.broadcast_to(rows_a[u : u + 1, :], (16, rank)).astype(bf16)
            mixed.append((rows_b.reshape(BLK // 16, 16, rank) * row[None]).reshape(BLK, rank))
        mixed = jnp.concatenate(mixed, 0)
        return mixed, lax.dot_general(mixed, rows_c, (((1,), (1,)), ((), ())), preferred_element_type=f32)

    sum_b = sum_c = jnp.zeros((BLK, rank), f32)
    parts = []
    later = start(0)
    for first in range(0, BLK, GROUP):
        mixed, rate = later
        if first + GROUP < BLK:
            later = start(first + GROUP)
        error = []
        for i in range(GROUP):
            seen = held[first + i].astype(f32)
            one = (jnp.exp(rate[i * BLK : (i + 1) * BLK]) - seen).astype(bf16)
            error.append(one * weight[:, first + i : first + i + 1])
        error = jnp.concatenate(error, 0)
        spread = jnp.dot(error, rows_c, preferred_element_type=f32)
        for i in range(GROUP):
            mine = spread[i * BLK : (i + 1) * BLK]
            sum_b = sum_b + mine * rows_a[first + i : first + i + 1, :]
            parts.append(jnp.sum(mine * wide_b, 0, keepdims=True))
        sum_c = sum_c + lax.dot_general(error, mixed, (((0,), (0,)), ((), ())), preferred_element_type=f32)
    grad_a[pl.ds(at_a, BLK), :] += jnp.concatenate(parts, 0)
    grad_b[pl.ds(at_b, BLK), :] += sum_b
    grad_c[pl.ds(at_c, BLK), :] += sum_c


def block_kernel(nx, ny, nz, table, entries, weights, early, *refs):
    along_z, along_x, rest_b, got_ac = take(refs, nz, nx, nx - 1, ny)
    refs = refs[nz + 2 * nx - 1 + ny :]
    own_b, own_ac = refs[:2]
    send_b, send_ac = refs[2 : 1 + nx], refs[1 + nx : nx + ny]
    slab_a, slab_b, slab_c, grad_a, grad_b, grad_c, held, arrivals = refs[nx + ny :]
    x, y, z = (lax.axis_index(name) for name in ("gx", "gy", "gz"))
    all_a, all_b, all_c = (s.shape[0] for s in (slab_a, slab_b, slab_c))
    per_a, per_b, per_c = all_a // (ny * nz), all_b // (nx * nz), all_c // (nx * ny)
    count = table[0]

    def copy(slot, chunk):
        rows = pl.ds(chunk * CHUNK, CHUNK)
        return pltpu.make_async_copy(
            entries.at[0, 0, 0, slot, rows], held.at[slot - 1, rows], arrivals.at[slot - 1, chunk]
        )

    def fetch(slot):
        @pl.when(slot < count)
        def _():
            for chunk in range(BLK // CHUNK):
                copy(slot, chunk).start()

    fetch(1)
    grad_a[...] = jnp.zeros_like(grad_a)
    grad_b[...] = jnp.zeros_like(grad_b)
    grad_c[...] = jnp.zeros_like(grad_c)
    for j in range(nz):
        of_z = lax.rem(z + nz - j, nz)
        for i in range(nx):
            at = (lax.rem(x + nx - i, nx) * nz + of_z) * per_b
            if i == 0:
                rows = along_z[j][:per_b, :]
            elif j == 0:
                rows = along_x[i][per_c:, :]
            else:
                rows = rest_b[i - 1][(j - 1) * per_b : j * per_b, :]
            slab_b[pl.ds(pl.multiple_of(at, per_b), per_b), :] = rows
        for i in range(ny):
            at = (before(y, i, ny) * nz + of_z) * per_a
            slab_a[pl.ds(pl.multiple_of(at, per_a), per_a), :] = got_ac[i][j * per_a : (j + 1) * per_a, :]
    for j in range(nx):
        of_x = lax.rem(x + nx - j, nx)
        for i in range(ny):
            at = (of_x * ny + before(y, i, ny)) * per_c
            first = nz * per_a + j * per_c
            slab_c[pl.ds(pl.multiple_of(at, per_c), per_c), :] = got_ac[i][first : first + per_c, :]

    def add(slot, ready):
        places = [table[1 + 3 * slot + i] for i in range(3)]
        slabs, grads = (slab_a, slab_b, slab_c), (grad_a, grad_b, grad_c)
        add_block(places, weights[slot], slabs, grads, ready)

    @pl.when(count > 0)
    def _():
        add(0, early)

    @pl.loop(1, count)
    def _(slot):
        for chunk in range(BLK // CHUNK):
            copy(slot, chunk).wait()
        fetch(slot + 1)
        add(slot, held.at[slot - 1])

    some_b, some_a = all_b // nx, all_a // ny
    for i in range(nx):
        to_x = lax.rem(x + i, nx)
        part_b = grad_b[pl.ds(pl.multiple_of(to_x * some_b, some_b), some_b), :]
        if i == 0:
            own_b[...] = part_b
        else:
            pack((part_b,), send_b[i - 1])
    for i in range(ny):
        to_y = lax.rem(y + i, ny)
        part_a = grad_a[pl.ds(pl.multiple_of(to_y * some_a, some_a), some_a), :]
        part_c = jnp.concatenate(
            [grad_c[pl.ds(pl.multiple_of((j * ny + to_y) * per_c, per_c), per_c), :] for j in range(nx)], 0
        )
        if i == 0:
            own_ac[:some_a, :] = part_a
            own_ac[some_a:, :] = part_c
        else:
            pack((part_a, part_c), send_ac[i - 1])


def middle_kernel(nx, ny, nz, sizes, *refs):
    some_b, some_c, some_a = sizes
    own_b, own_ac = refs[:2]
    got_b, got_ac = refs[2 : 1 + nx], refs[1 + nx : nx + ny]
    own_ba, own_c = refs[nx + ny : nx + ny + 2]
    send_ba = refs[nx + ny + 2 : nx + ny + 1 + nz]
    send_c = refs[nx + ny + 1 + nz : 2 * nx + ny + nz]
    sum_b, sum_c, sum_a = refs[2 * nx + ny + nz :]
    x, z = lax.axis_index("gx"), lax.axis_index("gz")
    total_b, total_a, total_c = own_b[...], own_ac[:some_a, :], own_ac[some_a:, :]
    for ref in got_b:
        total_b = total_b + unpack(ref, (some_b,))[0]
    for ref in got_ac:
        part_a, part_c = unpack(ref, (some_a, some_c))
        total_a, total_c = total_a + part_a, total_c + part_c
    sum_b[...], sum_c[...], sum_a[...] = total_b, total_c, total_a
    per_b, per_c, per_a = some_b // nz, some_c // nx, some_a // nz
    for i in range(nz):
        to_z = lax.rem(z + i, nz)
        part_b = sum_b[pl.ds(pl.multiple_of(to_z * per_b, per_b), per_b), :]
        part_a = sum_a[pl.ds(pl.multiple_of(to_z * per_a, per_a), per_a), :]
        if i == 0:
            own_ba[:per_b, :] = part_b
            own_ba[per_b:, :] = part_a
        else:
            pack((part_b, part_a), send_ba[i - 1])
    for i in range(nx):
        to_x = lax.rem(x + i, nx)
        part_c = sum_c[pl.ds(pl.multiple_of(to_x * per_c, per_c), per_c), :]
        if i == 0:
            own_c[...] = part_c
        else:
            pack((part_c,), send_c[i - 1])


def last_kernel(nx, nz, sizes, *refs):
    per_b, per_c, per_a = sizes
    own_ba, own_c = refs[:2]
    got_ba, got_c = refs[2 : 1 + nz], refs[1 + nz : nz + nx]
    grad_a, grad_b, grad_c = refs[nz + nx :]
    total_b, total_a, total_c = own_ba[:per_b, :], own_ba[per_b:, :], own_c[...]
    for ref in got_ba:
        part_b, part_a = unpack(ref, (per_b, per_a))
        total_b, total_a = total_b + part_b, total_a + part_a
    for ref in got_c:
        total_c = total_c + unpack(ref, (per_c,))[0]
    grad_a[0] = total_a * (1.0 / BLK)
    grad_b[0] = total_b * (1.0 / BLK)
    grad_c[0] = total_c * (1.0 / BLK)


def shift(array, axis, size, by):
    return lax.ppermute(array, axis, [(i, (i + by) % size) for i in range(size)])


def around(array, axis, size):
    return [array] + [shift(array, axis, size, by) for by in range(1, size)]


def pairwise(array, axis, size):
    near = 2 - size % 2
    far = [array] + [shift(array, axis, size, by) for by in range(near, size, near)]
    if near == 1:
        return far
    swapped = [lax.ppermute(item, axis, [(i, i ^ 1) for i in range(size)]) for item in far]
    return [item for pair in zip(far, swapped) for item in pair]


def before(me, place, size):
    near = 2 - size % 2
    if place % near:
        me = me + 1 - 2 * lax.rem(me, 2)
    return lax.rem(me + size - place // near * near, size)


def per_device(nx, ny, nz, tensor_blocks, fiber_mask, block_coords, block_counts, factor_a, factor_b, factor_c):
    per_a, per_b, per_c = (f.shape[1] for f in (factor_a, factor_b, factor_c))
    rank = factor_a.shape[2]
    all_a, all_b, all_c = per_a * ny * nz, per_b * nx * nz, per_c * nx * ny
    some_a, some_b, some_c = per_a * nz, per_b * nz, per_c * nx
    slots = tensor_blocks.shape[3]

    along_z = around(jnp.concatenate([factor_b[0], factor_a[0]], 0), "gz", nz)
    weights = fiber_mask[0, 0, 0].astype(jnp.bfloat16)
    table = jnp.concatenate([block_counts.reshape(1), jnp.swapaxes(block_coords[0, 0, 0], 0, 1).reshape(3 * slots)])
    along_x = around(jnp.concatenate([factor_c[0], factor_b[0]], 0), "gx", nx)
    *along_z, weights, table = lax.optimization_barrier((*along_z, weights, table))
    some_ac = jnp.concatenate([p[per_b:] for p in along_z] + [p[:per_c] for p in along_x], 0)
    got_ac = pairwise(some_ac, "gy", ny)
    rest_b = around(jnp.concatenate([p[:per_b] for p in along_z[1:]], 0), "gx", nx)[1:]
    early = jnp.maximum(tensor_blocks[0, 0, 0, 0], 0)

    f32, i16 = jnp.float32, jnp.int16
    outs = [jax.ShapeDtypeStruct((some_b, rank), f32), jax.ShapeDtypeStruct((some_a + some_c, rank), f32)]
    outs += [jax.ShapeDtypeStruct((some_b + PAD, rank), i16)] * (nx - 1)
    outs += [jax.ShapeDtypeStruct((some_a + some_c + PAD, rank), i16)] * (ny - 1)
    results = pl.pallas_call(
        functools.partial(block_kernel, nx, ny, nz),
        in_specs=[pl.BlockSpec(memory_space=pltpu.SMEM), pl.BlockSpec(memory_space=pl.ANY)]
        + [pl.BlockSpec(memory_space=pltpu.VMEM)] * (1 + nz + 2 * nx + ny),
        scratch_shapes=[pltpu.VMEM((n, rank), jnp.bfloat16) for n in (all_a, all_b, all_c)]
        + [pltpu.VMEM((n, rank), f32) for n in (all_a, all_b, all_c)]
        + [pltpu.VMEM((slots - 1, BLK, BLK, BLK), jnp.bfloat16), pltpu.SemaphoreType.DMA((slots - 1, BLK // CHUNK))],
        out_shape=outs,
        compiler_params=pltpu.CompilerParams(vmem_limit_bytes=44 * 2**20),
        name="blocks",
    )(table, tensor_blocks, weights, early, *along_z, *along_x, *rest_b, *got_ac)

    own_b, own_ac = results[:2]
    got_b = [shift(r, "gx", nx, i + 1) for i, r in enumerate(results[2 : 1 + nx])]
    got_ac = [shift(r, "gy", ny, i + 1) for i, r in enumerate(results[1 + nx :])]
    outs = [jax.ShapeDtypeStruct((per_b + per_a, rank), f32), jax.ShapeDtypeStruct((per_c, rank), f32)]
    outs += [jax.ShapeDtypeStruct((per_b + per_a + PAD, rank), i16)] * (nz - 1)
    outs += [jax.ShapeDtypeStruct((per_c + PAD, rank), i16)] * (nx - 1)
    results = pl.pallas_call(
        functools.partial(middle_kernel, nx, ny, nz, (some_b, some_c, some_a)),
        out_shape=outs,
        scratch_shapes=[pltpu.VMEM((n, rank), f32) for n in (some_b, some_c, some_a)],
        compiler_params=pltpu.CompilerParams(vmem_limit_bytes=32 * 2**20),
        name="middle",
    )(own_b, own_ac, *got_b, *got_ac)

    own_ba, own_c = results[:2]
    got_ba = [shift(r, "gz", nz, i + 1) for i, r in enumerate(results[2 : 1 + nz])]
    got_c = [shift(r, "gx", nx, i + 1) for i, r in enumerate(results[1 + nz :])]
    return pl.pallas_call(
        functools.partial(last_kernel, nx, nz, (per_b, per_c, per_a)),
        out_shape=[jax.ShapeDtypeStruct((1, n, rank), f32) for n in (per_a, per_b, per_c)],
        compiler_params=pltpu.CompilerParams(vmem_limit_bytes=32 * 2**20),
        name="last",
    )(own_ba, own_c, *got_ba, *got_c)


def solution(mesh):
    nx, ny, nz = (mesh.shape[name] for name in ("gx", "gy", "gz"))
    placed = (
        P("gx", "gy", "gz", None, None, None, None),
        P("gx", "gy", "gz", None, None, None),
        P("gx", "gy", "gz", None, None),
        P("gx", "gy", "gz"),
        P("gx", ("gy", "gz"), None),
        P("gy", ("gx", "gz"), None),
        P("gz", ("gx", "gy"), None),
    )
    return jax.shard_map(
        functools.partial(per_device, nx, ny, nz),
        mesh=mesh,
        in_specs=placed,
        out_specs=(
            P("gx", ("gy", "gz"), None),
            P("gy", ("gx", "gz"), None),
            P("gz", ("gx", "gy"), None),
        ),
        check_vma=False,
    )
```

```python
import functools

import jax
import jax.numpy as jnp
from jax import lax
from jax.experimental import pallas as pl
from jax.experimental.pallas import tpu as pltpu
from jax.sharding import PartitionSpec as P

BLK = 128
CHUNK = 32
GROUP = 8
PAD = 16
TOP = 32000.0


def pack(parts, target):
    at, powers = 0, []
    for part in parts:
        largest = jnp.maximum(jnp.max(jnp.abs(part), 0, keepdims=True), 1e-33)
        power = jnp.clip(jnp.ceil(jnp.log2(largest * (1.0 / TOP))), -120.0, 120.0)
        values = jnp.round(part * jnp.exp2(-power)).astype(jnp.int32)
        target[at : at + part.shape[0], :] = values.astype(jnp.int16)
        powers.append(power.astype(jnp.int32))
        at += part.shape[0]
    fill = jnp.zeros((PAD - len(powers), powers[0].shape[1]), jnp.int32)
    target[at : at + PAD, :] = jnp.concatenate([*powers, fill], 0).astype(jnp.int16)


def unpack(source, sizes):
    at, parts = 0, []
    powers = source[sum(sizes) : sum(sizes) + PAD, :].astype(jnp.int32).astype(jnp.float32)
    for i, size in enumerate(sizes):
        values = source[at : at + size, :].astype(jnp.int32).astype(jnp.float32)
        parts.append(values * jnp.exp2(powers[i : i + 1, :]))
        at += size
    return parts


def take(items, *counts):
    runs = []
    for count in counts:
        runs.append(items[:count])
        items = items[count:]
    return runs


def add_block(places, weight, slabs, grads, held):
    slab_a, slab_b, slab_c = slabs
    grad_a, grad_b, grad_c = grads
    f32, bf16 = jnp.float32, jnp.bfloat16
    at_a, at_b, at_c = (pl.multiple_of(places[i] * BLK, BLK) for i in range(3))
    rows_a = slab_a[pl.ds(at_a, BLK), :].astype(f32)
    rows_b = slab_b[pl.ds(at_b, BLK), :]
    rows_c = slab_c[pl.ds(at_c, BLK), :]
    rank = rows_b.shape[1]
    wide_b = rows_b.astype(f32)
    weight = jnp.transpose(weight.astype(f32)).astype(bf16)

    def start(first):
        mixed = []
        for u in range(first, first + GROUP):
            row = jnp.broadcast_to(rows_a[u : u + 1, :], (16, rank)).astype(bf16)
            mixed.append((rows_b.reshape(BLK // 16, 16, rank) * row[None]).reshape(BLK, rank))
        mixed = jnp.concatenate(mixed, 0)
        return mixed, lax.dot_general(mixed, rows_c, (((1,), (1,)), ((), ())), preferred_element_type=f32)

    sum_b = sum_c = jnp.zeros((BLK, rank), f32)
    parts = []
    later = start(0)
    for first in range(0, BLK, GROUP):
        mixed, rate = later
        if first + GROUP < BLK:
            later = start(first + GROUP)
        error = []
        for i in range(GROUP):
            seen = held[first + i].astype(f32)
            one = (jnp.exp(rate[i * BLK : (i + 1) * BLK]) - seen).astype(bf16)
            error.append(one * weight[:, first + i : first + i + 1])
        error = jnp.concatenate(error, 0)
        spread = jnp.dot(error, rows_c, preferred_element_type=f32)
        for i in range(GROUP):
            mine = spread[i * BLK : (i + 1) * BLK]
            sum_b = sum_b + mine * rows_a[first + i : first + i + 1, :]
            parts.append(jnp.sum(mine * wide_b, 0, keepdims=True))
        sum_c = sum_c + lax.dot_general(error, mixed, (((0,), (0,)), ((), ())), preferred_element_type=f32)
    grad_a[pl.ds(at_a, BLK), :] += jnp.concatenate(parts, 0)
    grad_b[pl.ds(at_b, BLK), :] += sum_b
    grad_c[pl.ds(at_c, BLK), :] += sum_c


def block_kernel(nx, ny, nz, table, entries, weights, early, *refs):
    along_z, along_x, rest_b, got_ac = take(refs, nz, nx, nx - 1, ny)
    refs = refs[nz + 2 * nx - 1 + ny :]
    own_b, own_ac = refs[:2]
    send_b, send_ac = refs[2 : 1 + nx], refs[1 + nx : nx + ny]
    slab_a, slab_b, slab_c, grad_a, grad_b, grad_c, held, arrivals = refs[nx + ny :]
    x, y, z = (lax.axis_index(name) for name in ("gx", "gy", "gz"))
    all_a, all_b, all_c = (s.shape[0] for s in (slab_a, slab_b, slab_c))
    per_a, per_b, per_c = all_a // (ny * nz), all_b // (nx * nz), all_c // (nx * ny)
    count = table[0]

    def copy(slot, chunk):
        rows = pl.ds(chunk * CHUNK, CHUNK)
        return pltpu.make_async_copy(
            entries.at[0, 0, 0, slot, rows], held.at[slot - 1, rows], arrivals.at[slot - 1, chunk]
        )

    def fetch(slot):
        @pl.when(slot < count)
        def _():
            for chunk in range(BLK // CHUNK):
                copy(slot, chunk).start()

    fetch(1)
    grad_a[...] = jnp.zeros_like(grad_a)
    grad_b[...] = jnp.zeros_like(grad_b)
    grad_c[...] = jnp.zeros_like(grad_c)
    for j in range(nz):
        of_z = lax.rem(z + nz - j, nz)
        for i in range(nx):
            at = (lax.rem(x + nx - i, nx) * nz + of_z) * per_b
            if i == 0:
                rows = along_z[j][:per_b, :]
            elif j == 0:
                rows = along_x[i][per_c:, :]
            else:
                rows = rest_b[i - 1][(j - 1) * per_b : j * per_b, :]
            slab_b[pl.ds(pl.multiple_of(at, per_b), per_b), :] = rows
        for i in range(ny):
            at = (before(y, i, ny) * nz + of_z) * per_a
            slab_a[pl.ds(pl.multiple_of(at, per_a), per_a), :] = got_ac[i][j * per_a : (j + 1) * per_a, :]
    for j in range(nx):
        of_x = lax.rem(x + nx - j, nx)
        for i in range(ny):
            at = (of_x * ny + before(y, i, ny)) * per_c
            first = nz * per_a + j * per_c
            slab_c[pl.ds(pl.multiple_of(at, per_c), per_c), :] = got_ac[i][first : first + per_c, :]

    def add(slot, ready):
        places = [table[1 + 3 * slot + i] for i in range(3)]
        slabs, grads = (slab_a, slab_b, slab_c), (grad_a, grad_b, grad_c)
        add_block(places, weights[slot], slabs, grads, ready)

    @pl.when(count > 0)
    def _():
        add(0, early)

    @pl.loop(1, count)
    def _(slot):
        for chunk in range(BLK // CHUNK):
            copy(slot, chunk).wait()
        fetch(slot + 1)
        add(slot, held.at[slot - 1])

    some_b, some_a = all_b // nx, all_a // ny
    for i in range(nx):
        to_x = lax.rem(x + i, nx)
        part_b = grad_b[pl.ds(pl.multiple_of(to_x * some_b, some_b), some_b), :]
        if i == 0:
            own_b[...] = part_b
        else:
            pack((part_b,), send_b[i - 1])
    for i in range(ny):
        to_y = lax.rem(y + i, ny)
        part_a = grad_a[pl.ds(pl.multiple_of(to_y * some_a, some_a), some_a), :]
        part_c = jnp.concatenate(
            [grad_c[pl.ds(pl.multiple_of((j * ny + to_y) * per_c, per_c), per_c), :] for j in range(nx)], 0
        )
        if i == 0:
            own_ac[:some_a, :] = part_a
            own_ac[some_a:, :] = part_c
        else:
            pack((part_a, part_c), send_ac[i - 1])


def middle_kernel(nx, ny, nz, sizes, *refs):
    some_b, some_c, some_a = sizes
    own_b, own_ac = refs[:2]
    got_b, got_ac = refs[2 : 1 + nx], refs[1 + nx : nx + ny]
    own_ba, own_c = refs[nx + ny : nx + ny + 2]
    send_ba = refs[nx + ny + 2 : nx + ny + 1 + nz]
    send_c = refs[nx + ny + 1 + nz : 2 * nx + ny + nz]
    sum_b, sum_c, sum_a = refs[2 * nx + ny + nz :]
    x, z = lax.axis_index("gx"), lax.axis_index("gz")
    total_b, total_a, total_c = own_b[...], own_ac[:some_a, :], own_ac[some_a:, :]
    for ref in got_b:
        total_b = total_b + unpack(ref, (some_b,))[0]
    for ref in got_ac:
        part_a, part_c = unpack(ref, (some_a, some_c))
        total_a, total_c = total_a + part_a, total_c + part_c
    sum_b[...], sum_c[...], sum_a[...] = total_b, total_c, total_a
    per_b, per_c, per_a = some_b // nz, some_c // nx, some_a // nz
    for i in range(nz):
        to_z = lax.rem(z + i, nz)
        part_b = sum_b[pl.ds(pl.multiple_of(to_z * per_b, per_b), per_b), :]
        part_a = sum_a[pl.ds(pl.multiple_of(to_z * per_a, per_a), per_a), :]
        if i == 0:
            own_ba[:per_b, :] = part_b
            own_ba[per_b:, :] = part_a
        else:
            pack((part_b, part_a), send_ba[i - 1])
    for i in range(nx):
        to_x = lax.rem(x + i, nx)
        part_c = sum_c[pl.ds(pl.multiple_of(to_x * per_c, per_c), per_c), :]
        if i == 0:
            own_c[...] = part_c
        else:
            pack((part_c,), send_c[i - 1])


def last_kernel(nx, nz, sizes, *refs):
    per_b, per_c, per_a = sizes
    own_ba, own_c = refs[:2]
    got_ba, got_c = refs[2 : 1 + nz], refs[1 + nz : nz + nx]
    grad_a, grad_b, grad_c = refs[nz + nx :]
    total_b, total_a, total_c = own_ba[:per_b, :], own_ba[per_b:, :], own_c[...]
    for ref in got_ba:
        part_b, part_a = unpack(ref, (per_b, per_a))
        total_b, total_a = total_b + part_b, total_a + part_a
    for ref in got_c:
        total_c = total_c + unpack(ref, (per_c,))[0]
    grad_a[0] = total_a * (1.0 / BLK)
    grad_b[0] = total_b * (1.0 / BLK)
    grad_c[0] = total_c * (1.0 / BLK)


def shift(array, axis, size, by):
    return lax.ppermute(array, axis, [(i, (i + by) % size) for i in range(size)])


def around(array, axis, size):
    return [array] + [shift(array, axis, size, by) for by in range(1, size)]


def pairwise(array, axis, size, meanwhile):
    near = 2 - size % 2
    far = [array] + [shift(array, axis, size, by) for by in range(near, size, near)]
    if near == 1:
        return far, meanwhile
    own, meanwhile = lax.optimization_barrier((array, meanwhile))
    swapped = [lax.ppermute(item, axis, [(i, i ^ 1) for i in range(size)]) for item in [own] + far[1:]]
    return [item for pair in zip(far, swapped) for item in pair], meanwhile


def before(me, place, size):
    near = 2 - size % 2
    if place % near:
        me = me + 1 - 2 * lax.rem(me, 2)
    return lax.rem(me + size - place // near * near, size)


def per_device(nx, ny, nz, tensor_blocks, fiber_mask, block_coords, block_counts, factor_a, factor_b, factor_c):
    per_a, per_b, per_c = (f.shape[1] for f in (factor_a, factor_b, factor_c))
    rank = factor_a.shape[2]
    all_a, all_b, all_c = per_a * ny * nz, per_b * nx * nz, per_c * nx * ny
    some_a, some_b, some_c = per_a * nz, per_b * nz, per_c * nx
    slots = tensor_blocks.shape[3]

    along_z = around(jnp.concatenate([factor_b[0], factor_a[0]], 0), "gz", nz)
    weights = fiber_mask[0, 0, 0].astype(jnp.bfloat16)
    table = jnp.concatenate([block_counts.reshape(1), jnp.swapaxes(block_coords[0, 0, 0], 0, 1).reshape(3 * slots)])
    along_x = around(jnp.concatenate([factor_c[0], factor_b[0]], 0), "gx", nx)
    *along_z, weights, table = lax.optimization_barrier((*along_z, weights, table))
    some_ac = jnp.concatenate([p[per_b:] for p in along_z] + [p[:per_c] for p in along_x], 0)
    early = jnp.maximum(tensor_blocks[0, 0, 0, 0], 0)
    got_ac, early = pairwise(some_ac, "gy", ny, early)
    rest_b = around(jnp.concatenate([p[:per_b] for p in along_z[1:]], 0), "gx", nx)[1:]

    f32, i16 = jnp.float32, jnp.int16
    outs = [jax.ShapeDtypeStruct((some_b, rank), f32), jax.ShapeDtypeStruct((some_a + some_c, rank), f32)]
    outs += [jax.ShapeDtypeStruct((some_b + PAD, rank), i16)] * (nx - 1)
    outs += [jax.ShapeDtypeStruct((some_a + some_c + PAD, rank), i16)] * (ny - 1)
    results = pl.pallas_call(
        functools.partial(block_kernel, nx, ny, nz),
        in_specs=[pl.BlockSpec(memory_space=pltpu.SMEM), pl.BlockSpec(memory_space=pl.ANY)]
        + [pl.BlockSpec(memory_space=pltpu.VMEM)] * (1 + nz + 2 * nx + ny),
        scratch_shapes=[pltpu.VMEM((n, rank), jnp.bfloat16) for n in (all_a, all_b, all_c)]
        + [pltpu.VMEM((n, rank), f32) for n in (all_a, all_b, all_c)]
        + [pltpu.VMEM((slots - 1, BLK, BLK, BLK), jnp.bfloat16), pltpu.SemaphoreType.DMA((slots - 1, BLK // CHUNK))],
        out_shape=outs,
        compiler_params=pltpu.CompilerParams(vmem_limit_bytes=44 * 2**20),
        name="blocks",
    )(table, tensor_blocks, weights, early, *along_z, *along_x, *rest_b, *got_ac)

    own_b, own_ac = results[:2]
    got_b = [shift(r, "gx", nx, i + 1) for i, r in enumerate(results[2 : 1 + nx])]
    got_ac = [shift(r, "gy", ny, i + 1) for i, r in enumerate(results[1 + nx :])]
    outs = [jax.ShapeDtypeStruct((per_b + per_a, rank), f32), jax.ShapeDtypeStruct((per_c, rank), f32)]
    outs += [jax.ShapeDtypeStruct((per_b + per_a + PAD, rank), i16)] * (nz - 1)
    outs += [jax.ShapeDtypeStruct((per_c + PAD, rank), i16)] * (nx - 1)
    results = pl.pallas_call(
        functools.partial(middle_kernel, nx, ny, nz, (some_b, some_c, some_a)),
        out_shape=outs,
        scratch_shapes=[pltpu.VMEM((n, rank), f32) for n in (some_b, some_c, some_a)],
        compiler_params=pltpu.CompilerParams(vmem_limit_bytes=32 * 2**20),
        name="middle",
    )(own_b, own_ac, *got_b, *got_ac)

    own_ba, own_c = results[:2]
    got_ba = [shift(r, "gz", nz, i + 1) for i, r in enumerate(results[2 : 1 + nz])]
    got_c = [shift(r, "gx", nx, i + 1) for i, r in enumerate(results[1 + nz :])]
    return pl.pallas_call(
        functools.partial(last_kernel, nx, nz, (per_b, per_c, per_a)),
        out_shape=[jax.ShapeDtypeStruct((1, n, rank), f32) for n in (per_a, per_b, per_c)],
        compiler_params=pltpu.CompilerParams(vmem_limit_bytes=32 * 2**20),
        name="last",
    )(own_ba, own_c, *got_ba, *got_c)


def solution(mesh):
    nx, ny, nz = (mesh.shape[name] for name in ("gx", "gy", "gz"))
    placed = (
        P("gx", "gy", "gz", None, None, None, None),
        P("gx", "gy", "gz", None, None, None),
        P("gx", "gy", "gz", None, None),
        P("gx", "gy", "gz"),
        P("gx", ("gy", "gz"), None),
        P("gy", ("gx", "gz"), None),
        P("gz", ("gx", "gy"), None),
    )
    return jax.shard_map(
        functools.partial(per_device, nx, ny, nz),
        mesh=mesh,
        in_specs=placed,
        out_specs=(
            P("gx", ("gy", "gz"), None),
            P("gy", ("gx", "gz"), None),
            P("gz", ("gx", "gy"), None),
        ),
        check_vma=False,
    )
```
